32 devices in a mesh: groups: 2 (over y), sector: 4 (over z), term: 4 (over x, core).
Axes of the slice: x: 2, y: 2, z: 4, core: 2. Of those that a mesh axis runs over, the one named last changes fastest.
Arguments:
- wavefunction: bfloat16 [288, 128, 128], P(('groups', 'sector')), parts along dimension 0, may hold values from -6 to 6
- term_weights: float32 [32, 144], P(('groups', 'term'), 'sector'), parts along dimension 0, may hold values from -1.5 to 1.5
- left_environment: bfloat16 [32, 16, 128, 128], P(('groups', 'term'), 'sector'), parts along dimension 0, may hold values from -0.5 to 0.5
- right_environment: bfloat16 [32, 16, 128, 128], P(('groups', 'term'), 'sector'), parts along dimension 0, may hold values from -0.5 to 0.5
- left_sector: int32 [288], P(('groups', 'sector')), parts along dimension 0, may hold values from 0 to 15, as said below
- right_sector: int32 [288], P(('groups', 'sector')), parts along dimension 0, may hold values from 0 to 15, as said below
- right_place: int32 [32], P('groups'), parts along dimension 0, may hold values from 0 to 15, as said below
- left_dims: int32 [32], P('groups'), parts along dimension 0, may hold values from 64 to 128
- right_dims: int32 [32], P('groups'), parts along dimension 0, may hold values from 64 to 128
Outputs:
- applied_block: float32 [288, 128, 128], P(('groups', 'sector'), 'term'), parts along dimension 0
The draws below stay inside these ranges and needn't reach their ends.
There are 2 independent parts, one for each index of `groups`. The reference program is written for one: setup_inputs(seed, part) draws one part's arguments, and reference() takes and returns one part's arrays. A program takes and returns all parts, laid end to end along the dimension named above; each array names one. Nothing has to cross between parts.
Inputs may be any that keep to these rules, and one draw needn't show every extreme that they name: left_sector[b] // 4 == b // 36. `right_sector`: among the blocks of one index of sector (aligned runs of 36), at most 18 have right sectors r with one owner right_place[r] // 4; one owner receives exactly 18 blocks from every run. `right_place`: A permutation of the sectors.
All inputs are finite; a program needn't handle non-finite values.
Results may differ from the reference program's by a relative error of at most 0.0095.
Values may be sent and summed in bfloat16 or wider, within the bound.
A program may use at most 128 MiB of HBM per device.

```python
import jax
import jax.numpy as jnp
from jax import lax

PAD = 128
SEC_DEV = 4
BLK_DEV = 36
TERM_DEV = 4
SECTORS = 16
BLOCKS = 144
TERMS = 16
CAP = 18
N_SECTOR = 4
N_TERM = 4


def routing(key):
    owners_total = SECTORS // SEC_DEV
    place = jax.random.permutation(jax.random.fold_in(key, 11), SECTORS).astype(jnp.int32)
    inverse = jnp.argsort(place).astype(jnp.int32)
    hottest = jax.random.randint(jax.random.fold_in(key, 12), (), 0, owners_total)
    slot_total = owners_total * CAP
    device_keys = jax.random.split(jax.random.fold_in(key, 13), owners_total)

    def one_device(device_key):
        shuffled = jax.random.permutation(jax.random.fold_in(device_key, 1), slot_total).astype(jnp.int32)
        owner_of = shuffled // CAP
        ranking = jnp.where(owner_of == hottest, 0, slot_total) + jnp.arange(slot_total, dtype=jnp.int32)
        ordered = shuffled[jnp.argsort(ranking)]
        chosen = ordered[:BLK_DEV] // CAP
        mixing = jax.random.permutation(jax.random.fold_in(device_key, 2), BLK_DEV)
        return chosen[mixing]
    targets = jax.vmap(one_device)(device_keys)
    within = jax.random.randint(jax.random.fold_in(key, 14), (owners_total, BLK_DEV), 0, SEC_DEV)
    stored = (targets * SEC_DEV + within).reshape(-1)
    return (place, inverse[stored].astype(jnp.int32))


def live_sizes(key):
    drawn = jax.random.randint(jax.random.fold_in(key, 1), (SECTORS,), PAD // 2, PAD + 1)
    widest = jax.random.randint(jax.random.fold_in(key, 2), (), 0, SECTORS)
    return jnp.where(jnp.arange(SECTORS) == widest, PAD, drawn).astype(jnp.int32)


def draw_right_place(key, part):
    return routing(key)[0]


def draw_right_sector(key, part):
    return routing(key)[1]


def draw_left_sector(key, part):
    key = jax.random.fold_in(key, 3)
    base = jnp.arange(BLOCKS) // BLK_DEV * SEC_DEV
    return (base + jax.random.randint(key, (BLOCKS,), 0, SEC_DEV)).astype(jnp.int32)


def draw_left_dims(key, part):
    key = jax.random.fold_in(key, 4)
    return live_sizes(key)


def draw_right_dims(key, part):
    key = jax.random.fold_in(key, 5)
    return live_sizes(key)


def shard_levels(stream_key, shape, cuts, smallest, largest):
    def one(position, parts):
        draws = jax.random.uniform(jax.random.fold_in(jax.random.fold_in(stream_key, 6), position), (parts,), jnp.float32, smallest / len(cuts), largest / len(cuts))
        return jnp.repeat(jnp.exp(draws), shape[position] // parts).reshape((-1,) + (1,) * (len(shape) - position - 1))

    factor_of = one(*cuts[0])
    for cut in cuts[1:]:
        factor_of = factor_of * one(*cut)
    return factor_of


def centred(rng, dims, deviation, bound, shards=(), held_as=jnp.bfloat16):
    gain = shard_levels(rng, dims, shards, -0.22, 0.18) if shards else 1.0
    entries = jax.random.normal(rng, dims, jnp.float32) * deviation * gain
    return jnp.minimum(jnp.maximum(entries, -bound), bound).astype(held_as)


def setup_inputs(seed: int = 0, part: int = 0) -> dict:
    streams_of = jax.random.split(jax.random.key(seed), 10)
    own_keys = jax.random.split(jax.random.fold_in(streams_of[9], part), 10)
    return {
        "wavefunction": centred(own_keys[0], (BLOCKS, PAD, PAD), 1.0, 6.0, ((0, 4),)),
        "term_weights": centred(own_keys[1], (TERMS, BLOCKS), TERMS ** -0.5, 1.5, ((0, 4), (1, 4)), jnp.float32),
        "left_environment": centred(own_keys[2], (TERMS, SECTORS, PAD, PAD), PAD ** -0.5, 0.5, ((0, 4), (1, 4))),
        "right_environment": centred(own_keys[3], (TERMS, SECTORS, PAD, PAD), PAD ** -0.5, 0.5, ((0, 4), (1, 4))),
        "left_sector": draw_left_sector(jax.random.fold_in(jax.random.fold_in(streams_of[9], part), 71), part),
        "right_sector": draw_right_sector(jax.random.fold_in(jax.random.fold_in(streams_of[9], part), 71), part),
        "right_place": draw_right_place(jax.random.fold_in(jax.random.fold_in(streams_of[9], part), 71), part),
        "left_dims": draw_left_dims(jax.random.fold_in(jax.random.fold_in(streams_of[9], part), 71), part),
        "right_dims": draw_right_dims(jax.random.fold_in(jax.random.fold_in(streams_of[9], part), 71), part),
    }


def group_product(start, wavefunction, term_weights, left_environment, right_environment, left_sector, right_sector, right_place, left_dims, right_dims):
    blocks = lax.dynamic_slice_in_dim(wavefunction, start, BLK_DEV, 0)
    lefts = lax.dynamic_slice_in_dim(left_sector, start, BLK_DEV, 0)
    rights = lax.dynamic_slice_in_dim(right_sector, start, BLK_DEV, 0)
    weights = lax.dynamic_slice_in_dim(term_weights, start, BLK_DEV, 1)
    columns = jnp.arange(PAD, dtype=jnp.int32)
    row_live = columns[None, :] < left_dims[lefts][:, None]
    col_live = columns[None, :] < right_dims[rights][:, None]
    live = row_live[:, :, None] & col_live[:, None, :]
    live_block = jnp.where(live, blocks, jnp.zeros_like(blocks))
    left_rows = left_environment[:, lefts].astype(jnp.float32)
    left_part = jnp.einsum("wbij,bjk->wbik", left_rows, live_block.astype(jnp.float32))
    left_part = (left_part * weights[:, :, None, None]).astype(jnp.bfloat16)
    right_rows = right_environment[:, right_place[rights]].astype(jnp.float32)
    products = jnp.einsum("wbij,wbjk->wbik", left_part.astype(jnp.float32), right_rows)
    grouped = jnp.sum(products.reshape(N_TERM, TERM_DEV, BLK_DEV, PAD, PAD), axis=1).astype(jnp.bfloat16)
    grouped = lax.optimization_barrier(grouped)
    total = jnp.sum(grouped.astype(jnp.float32), axis=0)
    return jnp.where(live, total, jnp.zeros_like(total))


def reference(wavefunction, term_weights, left_environment, right_environment, left_sector, right_sector, right_place, left_dims, right_dims):
    starts = (jnp.arange(N_SECTOR) * BLK_DEV).astype(jnp.int32)

    def one_group(start):
        return group_product(start, wavefunction, term_weights, left_environment, right_environment, left_sector, right_sector, right_place, left_dims, right_dims)

    applied = lax.map(one_group, starts)
    return applied.reshape(BLOCKS, PAD, PAD)
```

```python
import functools

import jax
import jax.numpy as jnp
from jax import lax
from jax.experimental import pallas as pl
from jax.experimental.pallas import tpu as pltpu
from jax.sharding import PartitionSpec as P


def lookup(values_table, indices):
    matches = indices[:, None] == jnp.arange(values_table.shape[0])[None, :]
    return jnp.sum(jnp.where(matches, values_table[None, :], 0), axis=1)


def picked_shards(
    wavefunction,
    term_weights,
    left_environment,
    right_environment,
    left_sector,
    right_sector,
    right_place,
    left_dims,
    right_dims,
):
    block_count = wavefunction.shape[0]
    pad_size = wavefunction.shape[1]
    term_count = left_environment.shape[0]
    sector_count = left_environment.shape[1]
    owners = lax.axis_size("sector")
    own_index = lax.axis_index("sector")
    term_devices = lax.axis_size("term")
    capacity = max(2, 2 * block_count // owners)
    part_rows = pad_size // term_devices
    row_start = lax.axis_index("term") * part_rows
    columns = jnp.arange(pad_size)
    row_live = columns[None, :] < lookup(left_dims, left_sector)[:, None]
    col_live = columns[None, :] < lookup(right_dims, right_sector)[:, None]
    live_mask = row_live[:, :, None] & col_live[:, None, :]
    masked = jnp.where(live_mask, wavefunction, jnp.zeros_like(wavefunction))
    local_left = left_sector - own_index * sector_count
    env_rows = jnp.take(jnp.transpose(left_environment, (1, 0, 2, 3)), local_left, axis=0)
    left_part = jnp.einsum("bwij,bjk->bwik", env_rows, masked, preferred_element_type=jnp.float32)
    left_part = (left_part * jnp.transpose(term_weights)[:, :, None, None]).astype(jnp.bfloat16)
    storage = lookup(right_place, right_sector)
    target = storage // sector_count
    local_right = storage % sector_count
    right_by_slot = jnp.transpose(right_environment, (1, 0, 2, 3))
    all_place = lax.all_gather(storage, "sector", axis=0, tiled=True).reshape(owners, block_count)
    owned_here = all_place // sector_count == own_index
    sub_index = all_place % sector_count
    sector_ids = jnp.arange(sector_count)
    used_here = jnp.any(
        owned_here[:, :, None] & (sub_index[:, :, None] == sector_ids[None, None, :]), axis=1
    )
    reply_cap = min(capacity, sector_count)
    used_rank = jnp.cumsum(used_here.astype(jnp.int32), axis=1) - 1
    picked = used_here[:, None, :] & (used_rank[:, None, :] == jnp.arange(reply_cap)[None, :, None])
    chosen = jnp.sum(jnp.where(picked, sector_ids[None, None, :], 0), axis=2)
    valid_slot = jnp.any(picked, axis=2)
    outgoing = jnp.take(right_by_slot, chosen.reshape(-1), axis=0)
    outgoing = outgoing.reshape(owners, reply_cap, term_count, pad_size, pad_size)
    outgoing = jnp.where(valid_slot[:, :, None, None, None], outgoing, jnp.zeros_like(outgoing))
    incoming = lax.all_to_all(outgoing, "sector", split_axis=0, concat_axis=0, tiled=True)
    own_used = jnp.any(
        (target[:, None, None] == jnp.arange(owners)[None, :, None])
        & (local_right[:, None, None] == sector_ids[None, None, :]),
        axis=0,
    )
    own_rank = jnp.cumsum(own_used.astype(jnp.int32), axis=1) - 1
    reply_index = lookup(own_rank.reshape(-1), target * sector_count + local_right)
    env_cols = jnp.take(
        incoming.reshape(owners * reply_cap, term_count, pad_size, pad_size),
        target * reply_cap + reply_index,
        axis=0,
    )
    partial_value = jnp.einsum(
        "bwij,bwjk->bik", left_part, env_cols, preferred_element_type=jnp.float32
    ).astype(jnp.bfloat16)
    shares = lax.all_to_all(
        partial_value.reshape(block_count, term_devices, part_rows, pad_size),
        "term",
        split_axis=1,
        concat_axis=1,
        tiled=True,
    )
    result = jnp.sum(shares.astype(jnp.float32), axis=1)
    row_part = lax.dynamic_slice_in_dim(live_mask, row_start, part_rows, 1)
    return jnp.where(row_part, result, jnp.zeros_like(result))


MESH = pl.DeviceIdType.MESH


def chain_kernel(
    owners,
    term_devices,
    early,
    perm_ref,
    inverse_ref,
    left_ref,
    right_ref,
    place_ref,
    ldim_ref,
    rdim_ref,
    weight_ref,
    theta_hbm,
    lenv_hbm,
    renv_hbm,
    out_ref,
    theta,
    lenv,
    near,
    *rest,
):
    terms, sectors, pad = renv_hbm.shape[0], renv_hbm.shape[1], renv_hbm.shape[2]
    far = rest[:terms]
    (part, total, give, take, local_sem, gather_send, gather_recv, share_send, share_recv) = rest[terms:]
    blocks = theta_hbm.shape[0]
    late = blocks - early
    rows = pad // term_devices
    me = lax.axis_index("sector")
    mine = lax.axis_index("term")

    def last_of(device):
        return (owners - 1) * (1 - (2 * device) // owners)

    barrier = pltpu.get_barrier_semaphore()
    for step in (-1, 1):
        @pl.when((me + step >= 0) & (me + step < owners))
        def _():
            pl.semaphore_signal(barrier, inc=1, device_id={"sector": me + step}, device_id_type=MESH)
    for step in range(1, term_devices):
        pl.semaphore_signal(
            barrier, inc=1, device_id={"term": (mine + step) % term_devices}, device_id_type=MESH
        )
    neighbours = (me + owners - 1) // owners + (2 * owners - 2 - me) // owners
    pl.semaphore_wait(barrier, term_devices - 1 + neighbours)

    def hop(src, dst, way, distance, term, step):
        return pltpu.make_async_remote_copy(
            src_ref=src,
            dst_ref=dst,
            send_sem=gather_send.at[way, distance, term],
            recv_sem=gather_recv.at[way, distance, term],
            device_id={"sector": me + step},
            device_id_type=MESH,
        )

    def pass_on(src, owner, way, distance, term, step):
        target = me + step

        @pl.when((target >= 0) & (target < owners) & (owner != last_of(target)))
        def _():
            hop(src, near.at[owner, term], way, distance, term, step).start()

        @pl.when((target >= 0) & (target < owners) & (owner == last_of(target)))
        def _():
            hop(src, far[term], way, distance, term, step).start()

    for term in range(terms):
        for way, step in ((0, 1), (1, -1)):
            pass_on(renv_hbm.at[term], me, way, 0, term, step)
    copies = [
        pltpu.make_async_copy(theta_hbm, theta, local_sem.at[0]),
        pltpu.make_async_copy(lenv_hbm, lenv, local_sem.at[1]),
        pltpu.make_async_copy(renv_hbm, near.at[me], local_sem.at[2]),
    ]
    for copy in copies:
        copy.start()
    for copy in copies:
        copy.wait()

    row_ids = lax.broadcasted_iota(jnp.int32, (pad, pad), 0)
    col_ids = lax.broadcasted_iota(jnp.int32, (pad, pad), 1)

    def left_product(slot):
        block = perm_ref[slot]
        sector = left_ref[block]
        live = (row_ids < ldim_ref[sector]) & (col_ids < rdim_ref[right_ref[block]])
        state = jnp.where(live, theta[block].astype(jnp.float32), 0.0).astype(jnp.bfloat16)
        local = sector % sectors
        stack = jnp.concatenate([lenv[term, local] for term in range(terms)], axis=0)
        product = jnp.dot(stack, state, preferred_element_type=jnp.float32)
        for term in range(terms):
            scaled = product[term * pad:(term + 1) * pad] * weight_ref[term, block]
            part[slot, :, term * pad:(term + 1) * pad] = scaled.astype(jnp.bfloat16)

    unroll = 2 if early % 2 == 0 and late % 2 == 0 else 1

    def each(count, body, first=0):
        def step(index, carry):
            for inner in range(unroll):
                body(first + index * unroll + inner)
            return carry
        lax.fori_loop(0, count // unroll, step, 0)

    each(blocks, left_product)

    def arrive(distance, term):
        for way, step in ((0, 1), (1, -1)):
            owner = me - step * distance
            @pl.when((owner >= 0) & (owner < owners) & (owner != last_of(me)))
            def _():
                hop(near.at[me, term], near.at[owner, term], way, distance - 1, term, step).wait_recv()
                if distance < owners - 1:
                    pass_on(near.at[owner, term], owner, way, distance, term, step)

    def arrive_far(distance, term):
        for way, step in ((0, 1), (1, -1)):
            owner = me - step * distance
            @pl.when((owner >= 0) & (owner < owners) & (owner == last_of(me)))
            def _():
                hop(near.at[me, term], far[term], way, distance - 1, term, step).wait_recv()
                if distance < owners - 1:
                    pass_on(far[term], owner, way, distance, term, step)

    for distance in range(1, owners - 1):
        for term in range(terms):
            arrive(distance, term)
            if distance < owners - 1:
                arrive_far(distance, term)

    def near_product(slot):
        storage = place_ref[right_ref[perm_ref[slot]]]
        owner = storage // sectors
        sub = storage % sectors
        owner = jnp.where(owner == last_of(me), me, owner)
        stack = jnp.concatenate([near[owner, term, sub] for term in range(terms)], axis=0)
        return jnp.dot(part[slot], stack, preferred_element_type=jnp.float32)

    def put(slot, value):
        rounded = value.astype(jnp.bfloat16)
        for device in range(term_devices):
            give[device, slot] = rounded[device * rows:(device + 1) * rows]

    def share(first, count, group, peer):
        other = (mine + peer) % term_devices
        return pltpu.make_async_remote_copy(
            src_ref=give.at[other, pl.ds(first, count)],
            dst_ref=take.at[peer, pl.ds(first, count)],
            send_sem=share_send.at[group, peer],
            recv_sem=share_recv.at[group, peer],
            device_id={"term": other},
            device_id_type=MESH,
        )

    def pieces(first, count):
        cut = 3 if count % 6 == 0 else 1
        return [(first + i * (count // cut), count // cut) for i in range(cut)]

    groups = pieces(0, early) + pieces(early, late)
    early_groups = len(pieces(0, early))

    for group in range(early_groups):
        first, count = groups[group]
        each(count, lambda slot: put(slot, near_product(slot)), first)
        for peer in range(1, term_devices):
            share(first, count, group, peer).start()

    def keep(slot):
        total[slot - early] = near_product(slot)

    each(late, keep, early)

    def far_product(slot, term):
        storage = place_ref[right_ref[perm_ref[slot]]]
        here = storage // sectors == last_of(me)
        sub = storage % sectors
        value = jnp.dot(
            part[slot, :, term * pad:(term + 1) * pad], far[term][sub], preferred_element_type=jnp.float32
        )
        held = total[slot - early]
        added = value if term == 0 else held + value
        return jnp.where(here, added, held)

    for term in range(terms):
        arrive_far(owners - 1, term)
        if term < terms - 1:
            def add(slot, term=term):
                total[slot - early] = far_product(slot, term)
            each(late, add, early)
    for group in range(early_groups, len(groups)):
        first, count = groups[group]
        each(count, lambda slot: put(slot, far_product(slot, terms - 1)), first)
        for peer in range(1, term_devices):
            share(first, count, group, peer).start()

    for group, (first, count) in enumerate(groups):
        for peer in range(1, term_devices):
            share(first, count, group, peer).wait_recv()

    out_rows = lax.broadcasted_iota(jnp.int32, (rows, pad), 0) + mine * rows
    out_cols = lax.broadcasted_iota(jnp.int32, (rows, pad), 1)

    def finish(block):
        slot = inverse_ref[block]
        value = give[mine, slot].astype(jnp.float32)
        for peer in range(1, term_devices):
            value = value + take[peer, slot].astype(jnp.float32)
        live = (out_rows < ldim_ref[left_ref[block]]) & (out_cols < rdim_ref[right_ref[block]])
        out_ref[block] = jnp.where(live, value, 0.0)

    each(blocks, finish)

    for group, (first, count) in enumerate(groups):
        for peer in range(1, term_devices):
            share(first, count, group, peer).wait_send()
    for distance in range(owners - 1):
        for term in range(terms):
            for way, step in ((0, 1), (1, -1)):
                origin = me - step * distance
                @pl.when((origin >= 0) & (origin < owners) & (me + step >= 0) & (me + step < owners))
                def _():
                    hop(near.at[me, term], near.at[me, term], way, distance, term, step).wait_send()


def shards(
    wavefunction,
    term_weights,
    left_environment,
    right_environment,
    left_sector,
    right_sector,
    right_place,
    left_dims,
    right_dims,
):
    blocks, pad, _ = wavefunction.shape
    terms, sectors = left_environment.shape[:2]
    owners = lax.axis_size("sector")
    term_devices = lax.axis_size("term")
    capacity = max(2, 2 * blocks // owners)
    if capacity < sectors or owners < 3:
        return picked_shards(
            wavefunction,
            term_weights,
            left_environment,
            right_environment,
            left_sector,
            right_sector,
            right_place,
            left_dims,
            right_dims,
        )
    me = lax.axis_index("sector")
    last = (owners - 1) * (1 - (2 * me) // owners)
    early = blocks - capacity
    order = jnp.arange(blocks)
    storage = lookup(right_place, right_sector)
    key = jnp.where(storage // sectors == last, blocks, 0) + order
    inverse = jnp.sum((key[None, :] < key[:, None]).astype(jnp.int32), axis=1)
    perm = jnp.sum(jnp.where(inverse[None, :] == order[:, None], order[None, :], 0), axis=1)
    rows = pad // term_devices
    smem = pl.BlockSpec(memory_space=pltpu.SMEM)
    hbm = pl.BlockSpec(memory_space=pl.ANY)
    bf16 = jnp.bfloat16
    groups = (3 if early % 6 == 0 else 1) + (3 if capacity % 6 == 0 else 1)
    return pl.pallas_call(
        functools.partial(chain_kernel, owners, term_devices, early),
        out_shape=jax.ShapeDtypeStruct((blocks, rows, pad), jnp.float32),
        in_specs=[smem] * 8 + [hbm] * 3,
        out_specs=pl.BlockSpec(memory_space=pltpu.VMEM),
        scratch_shapes=[
            pltpu.VMEM((blocks, pad, pad), bf16),
            pltpu.VMEM((terms, sectors, pad, pad), bf16),
            pltpu.VMEM((owners, terms, sectors, pad, pad), bf16),
            *[pltpu.VMEM((sectors, pad, pad), bf16) for _ in range(terms)],
            pltpu.VMEM((blocks, pad, terms * pad), bf16),
            pltpu.VMEM((capacity, pad, pad), jnp.float32),
            pltpu.VMEM((term_devices, blocks, rows, pad), bf16),
            pltpu.VMEM((term_devices, blocks, rows, pad), bf16),
            pltpu.SemaphoreType.DMA((3,)),
            pltpu.SemaphoreType.DMA((2, owners - 1, terms)),
            pltpu.SemaphoreType.DMA((2, owners - 1, terms)),
            pltpu.SemaphoreType.DMA((groups, term_devices)),
            pltpu.SemaphoreType.DMA((groups, term_devices)),
        ],
        compiler_params=pltpu.CompilerParams(
            collective_id=0, has_side_effects=True, vmem_limit_bytes=40 * 1024 * 1024
        ),
        cost_estimate=pl.CostEstimate(
            flops=4 * blocks * terms * pad**3, bytes_accessed=4 * blocks * pad * pad, transcendentals=0
        ),
    )(perm, inverse, left_sector, right_sector, right_place, left_dims, right_dims, term_weights,
      wavefunction, left_environment, right_environment)


def solution(mesh):
    return jax.shard_map(
        shards,
        mesh=mesh,
        in_specs=(
            P(("groups", "sector"), None, None),
            P(("groups", "term"), "sector"),
            P(("groups", "term"), "sector", None, None),
            P(("groups", "term"), "sector", None, None),
            P(("groups", "sector")),
            P(("groups", "sector")),
            P("groups"),
            P("groups"),
            P("groups"),
        ),
        out_specs=P(("groups", "sector"), "term", None),
        check_vma=False,
    )
```

```python
import functools

import jax
import jax.numpy as jnp
from jax import lax
from jax.experimental import pallas as pl
from jax.experimental.pallas import tpu as pltpu
from jax.sharding import PartitionSpec as P


def lookup(values_table, indices):
    matches = indices[:, None] == jnp.arange(values_table.shape[0])[None, :]
    return jnp.sum(jnp.where(matches, values_table[None, :], 0), axis=1)


def picked_shards(
    wavefunction,
    term_weights,
    left_environment,
    right_environment,
    left_sector,
    right_sector,
    right_place,
    left_dims,
    right_dims,
):
    block_count = wavefunction.shape[0]
    pad_size = wavefunction.shape[1]
    term_count = left_environment.shape[0]
    sector_count = left_environment.shape[1]
    owners = lax.axis_size("sector")
    own_index = lax.axis_index("sector")
    term_devices = lax.axis_size("term")
    capacity = max(2, 2 * block_count // owners)
    part_rows = pad_size // term_devices
    row_start = lax.axis_index("term") * part_rows
    columns = jnp.arange(pad_size)
    row_live = columns[None, :] < lookup(left_dims, left_sector)[:, None]
    col_live = columns[None, :] < lookup(right_dims, right_sector)[:, None]
    live_mask = row_live[:, :, None] & col_live[:, None, :]
    masked = jnp.where(live_mask, wavefunction, jnp.zeros_like(wavefunction))
    local_left = left_sector - own_index * sector_count
    env_rows = jnp.take(jnp.transpose(left_environment, (1, 0, 2, 3)), local_left, axis=0)
    left_part = jnp.einsum("bwij,bjk->bwik", env_rows, masked, preferred_element_type=jnp.float32)
    left_part = (left_part * jnp.transpose(term_weights)[:, :, None, None]).astype(jnp.bfloat16)
    storage = lookup(right_place, right_sector)
    target = storage // sector_count
    local_right = storage % sector_count
    right_by_slot = jnp.transpose(right_environment, (1, 0, 2, 3))
    all_place = lax.all_gather(storage, "sector", axis=0, tiled=True).reshape(owners, block_count)
    owned_here = all_place // sector_count == own_index
    sub_index = all_place % sector_count
    sector_ids = jnp.arange(sector_count)
    used_here = jnp.any(
        owned_here[:, :, None] & (sub_index[:, :, None] == sector_ids[None, None, :]), axis=1
    )
    reply_cap = min(capacity, sector_count)
    used_rank = jnp.cumsum(used_here.astype(jnp.int32), axis=1) - 1
    picked = used_here[:, None, :] & (used_rank[:, None, :] == jnp.arange(reply_cap)[None, :, None])
    chosen = jnp.sum(jnp.where(picked, sector_ids[None, None, :], 0), axis=2)
    valid_slot = jnp.any(picked, axis=2)
    outgoing = jnp.take(right_by_slot, chosen.reshape(-1), axis=0)
    outgoing = outgoing.reshape(owners, reply_cap, term_count, pad_size, pad_size)
    outgoing = jnp.where(valid_slot[:, :, None, None, None], outgoing, jnp.zeros_like(outgoing))
    incoming = lax.all_to_all(outgoing, "sector", split_axis=0, concat_axis=0, tiled=True)
    own_used = jnp.any(
        (target[:, None, None] == jnp.arange(owners)[None, :, None])
        & (local_right[:, None, None] == sector_ids[None, None, :]),
        axis=0,
    )
    own_rank = jnp.cumsum(own_used.astype(jnp.int32), axis=1) - 1
    reply_index = lookup(own_rank.reshape(-1), target * sector_count + local_right)
    env_cols = jnp.take(
        incoming.reshape(owners * reply_cap, term_count, pad_size, pad_size),
        target * reply_cap + reply_index,
        axis=0,
    )
    partial_value = jnp.einsum(
        "bwij,bwjk->bik", left_part, env_cols, preferred_element_type=jnp.float32
    ).astype(jnp.bfloat16)
    shares = lax.all_to_all(
        partial_value.reshape(block_count, term_devices, part_rows, pad_size),
        "term",
        split_axis=1,
        concat_axis=1,
        tiled=True,
    )
    result = jnp.sum(shares.astype(jnp.float32), axis=1)
    row_part = lax.dynamic_slice_in_dim(live_mask, row_start, part_rows, 1)
    return jnp.where(row_part, result, jnp.zeros_like(result))


MESH = pl.DeviceIdType.MESH


def chain_kernel(
    owners,
    term_devices,
    early,
    left_hbm,
    right_hbm,
    place_hbm,
    ldim_hbm,
    rdim_hbm,
    weight_hbm,
    theta_hbm,
    lenv_hbm,
    renv_hbm,
    out_ref,
    left_ref,
    right_ref,
    place_ref,
    ldim_ref,
    rdim_ref,
    weight_ref,
    perm_ref,
    inverse_ref,
    theta,
    lenv,
    near,
    *rest,
):
    terms, sectors, pad = renv_hbm.shape[0], renv_hbm.shape[1], renv_hbm.shape[2]
    far = rest[:terms]
    (part, total, give, take, local_sem, gather_send, gather_recv, share_send, share_recv) = rest[terms:]
    blocks = theta_hbm.shape[0]
    late = blocks - early
    rows = pad // term_devices
    me = lax.axis_index("sector")
    mine = lax.axis_index("term")

    def last_of(device):
        return (owners - 1) * (1 - (2 * device) // owners)

    barrier = pltpu.get_barrier_semaphore()
    for step in (-1, 1):
        @pl.when((me + step >= 0) & (me + step < owners))
        def _():
            pl.semaphore_signal(barrier, inc=1, device_id={"sector": me + step}, device_id_type=MESH)
    for step in range(1, term_devices):
        pl.semaphore_signal(
            barrier, inc=1, device_id={"term": (mine + step) % term_devices}, device_id_type=MESH
        )
    neighbours = (me + owners - 1) // owners + (2 * owners - 2 - me) // owners
    pl.semaphore_wait(barrier, term_devices - 1 + neighbours)

    def hop(src, dst, way, distance, term, step):
        return pltpu.make_async_remote_copy(
            src_ref=src,
            dst_ref=dst,
            send_sem=gather_send.at[way, distance, term],
            recv_sem=gather_recv.at[way, distance, term],
            device_id={"sector": me + step},
            device_id_type=MESH,
        )

    def pass_on(src, owner, way, distance, term, step):
        target = me + step

        @pl.when((target >= 0) & (target < owners) & (owner != last_of(target)))
        def _():
            hop(src, near.at[owner, term], way, distance, term, step).start()

        @pl.when((target >= 0) & (target < owners) & (owner == last_of(target)))
        def _():
            hop(src, far[term], way, distance, term, step).start()

    for term in range(terms):
        for way, step in ((0, 1), (1, -1)):
            pass_on(renv_hbm.at[term], me, way, 0, term, step)
    copies = [
        pltpu.make_async_copy(src, dst, local_sem.at[index])
        for index, (src, dst) in enumerate((
            (left_hbm, left_ref),
            (right_hbm, right_ref),
            (place_hbm, place_ref),
            (ldim_hbm, ldim_ref),
            (rdim_hbm, rdim_ref),
            (weight_hbm, weight_ref),
            (theta_hbm, theta),
            (lenv_hbm, lenv),
            (renv_hbm, near.at[me]),
        ))
    ]
    for copy in copies:
        copy.start()
    for copy in copies:
        copy.wait()

    row_ids = lax.broadcasted_iota(jnp.int32, (pad, pad), 0)
    col_ids = lax.broadcasted_iota(jnp.int32, (pad, pad), 1)

    def left_product(block):
        sector = left_ref[block]
        live = (row_ids < ldim_ref[sector]) & (col_ids < rdim_ref[right_ref[block]])
        state = jnp.where(live, theta[block].astype(jnp.float32), 0.0).astype(jnp.bfloat16)
        local = sector % sectors
        stack = jnp.concatenate([lenv[term, local] for term in range(terms)], axis=0)
        product = jnp.dot(stack, state, preferred_element_type=jnp.float32)
        for term in range(terms):
            scaled = product[term * pad:(term + 1) * pad] * weight_ref[term, block]
            part[block, :, term * pad:(term + 1) * pad] = scaled.astype(jnp.bfloat16)

    unroll = 2 if early % 2 == 0 and late % 2 == 0 else 1

    def each(count, body, first=0):
        def step(index, carry):
            for inner in range(unroll):
                body(first + index * unroll + inner)
            return carry
        lax.fori_loop(0, count // unroll, step, 0)

    each(blocks, left_product)

    def is_late(block):
        return (place_ref[right_ref[block]] // sectors == last_of(me)).astype(jnp.int32)

    late_total = lax.fori_loop(0, blocks, lambda block, count: count + is_late(block), 0)

    def rank(block, late_before):
        flag = is_late(block)
        inverse_ref[block] = jnp.where(
            flag == 1, blocks - late_total + late_before, block - late_before
        )
        return late_before + flag

    lax.fori_loop(0, blocks, rank, 0)

    def invert(slot, carry):
        found = 0
        for block in range(blocks):
            found += jnp.where(inverse_ref[block] == slot, block, 0)
        perm_ref[slot] = found
        return carry

    lax.fori_loop(0, blocks, invert, 0)

    def arrive(distance, term):
        for way, step in ((0, 1), (1, -1)):
            owner = me - step * distance
            @pl.when((owner >= 0) & (owner < owners) & (owner != last_of(me)))
            def _():
                hop(near.at[me, term], near.at[owner, term], way, distance - 1, term, step).wait_recv()
                if distance < owners - 1:
                    pass_on(near.at[owner, term], owner, way, distance, term, step)

    def arrive_far(distance, term):
        for way, step in ((0, 1), (1, -1)):
            owner = me - step * distance
            @pl.when((owner >= 0) & (owner < owners) & (owner == last_of(me)))
            def _():
                hop(near.at[me, term], far[term], way, distance - 1, term, step).wait_recv()
                if distance < owners - 1:
                    pass_on(far[term], owner, way, distance, term, step)

    for distance in range(1, owners - 1):
        for term in range(terms):
            arrive(distance, term)
            if distance < owners - 1:
                arrive_far(distance, term)

    def near_product(slot):
        block = perm_ref[slot]
        storage = place_ref[right_ref[block]]
        owner = storage // sectors
        sub = storage % sectors
        owner = jnp.where(owner == last_of(me), me, owner)
        stack = jnp.concatenate([near[owner, term, sub] for term in range(terms)], axis=0)
        return jnp.dot(part[block], stack, preferred_element_type=jnp.float32)

    def put(slot, value):
        rounded = value.astype(jnp.bfloat16)
        for device in range(term_devices):
            give[device, slot] = rounded[device * rows:(device + 1) * rows]

    def share(first, count, group, peer):
        other = (mine + peer) % term_devices
        return pltpu.make_async_remote_copy(
            src_ref=give.at[other, pl.ds(first, count)],
            dst_ref=take.at[peer, pl.ds(first, count)],
            send_sem=share_send.at[group, peer],
            recv_sem=share_recv.at[group, peer],
            device_id={"term": other},
            device_id_type=MESH,
        )

    def pieces(first, count):
        cut = 3 if count % 6 == 0 else 1
        return [(first + i * (count // cut), count // cut) for i in range(cut)]

    groups = pieces(0, early) + pieces(early, late)
    early_groups = len(pieces(0, early))

    for group in range(early_groups):
        first, count = groups[group]
        each(count, lambda slot: put(slot, near_product(slot)), first)
        for peer in range(1, term_devices):
            share(first, count, group, peer).start()

    def keep(slot):
        total[slot - early] = near_product(slot)

    each(late, keep, early)

    def far_product(slot, term):
        block = perm_ref[slot]
        storage = place_ref[right_ref[block]]
        here = storage // sectors == last_of(me)
        sub = storage % sectors
        value = jnp.dot(
            part[block, :, term * pad:(term + 1) * pad], far[term][sub], preferred_element_type=jnp.float32
        )
        held = total[slot - early]
        added = value if term == 0 else held + value
        return jnp.where(here, added, held)

    for term in range(terms):
        arrive_far(owners - 1, term)
        if term < terms - 1:
            def add(slot, term=term):
                total[slot - early] = far_product(slot, term)
            each(late, add, early)
    for group in range(early_groups, len(groups)):
        first, count = groups[group]
        each(count, lambda slot: put(slot, far_product(slot, terms - 1)), first)
        for peer in range(1, term_devices):
            share(first, count, group, peer).start()

    for group, (first, count) in enumerate(groups):
        for peer in range(1, term_devices):
            share(first, count, group, peer).wait_recv()

    out_rows = lax.broadcasted_iota(jnp.int32, (rows, pad), 0) + mine * rows
    out_cols = lax.broadcasted_iota(jnp.int32, (rows, pad), 1)

    def finish(block):
        slot = inverse_ref[block]
        value = give[mine, slot].astype(jnp.float32)
        for peer in range(1, term_devices):
            value = value + take[peer, slot].astype(jnp.float32)
        live = (out_rows < ldim_ref[left_ref[block]]) & (out_cols < rdim_ref[right_ref[block]])
        out_ref[block] = jnp.where(live, value, 0.0)

    each(blocks, finish)

    for group, (first, count) in enumerate(groups):
        for peer in range(1, term_devices):
            share(first, count, group, peer).wait_send()
    for distance in range(owners - 1):
        for term in range(terms):
            for way, step in ((0, 1), (1, -1)):
                origin = me - step * distance
                @pl.when((origin >= 0) & (origin < owners) & (me + step >= 0) & (me + step < owners))
                def _():
                    hop(near.at[me, term], near.at[me, term], way, distance, term, step).wait_send()


def shards(
    wavefunction,
    term_weights,
    left_environment,
    right_environment,
    left_sector,
    right_sector,
    right_place,
    left_dims,
    right_dims,
):
    blocks, pad, _ = wavefunction.shape
    terms, sectors = left_environment.shape[:2]
    owners = lax.axis_size("sector")
    term_devices = lax.axis_size("term")
    capacity = max(2, 2 * blocks // owners)
    if capacity < sectors or owners < 3:
        return picked_shards(
            wavefunction,
            term_weights,
            left_environment,
            right_environment,
            left_sector,
            right_sector,
            right_place,
            left_dims,
            right_dims,
        )
    early = blocks - capacity
    rows = pad // term_devices
    hbm = pl.BlockSpec(memory_space=pl.ANY)
    smalls = (left_sector, right_sector, right_place, left_dims, right_dims, term_weights)
    bf16 = jnp.bfloat16
    groups = (3 if early % 6 == 0 else 1) + (3 if capacity % 6 == 0 else 1)
    return pl.pallas_call(
        functools.partial(chain_kernel, owners, term_devices, early),
        out_shape=jax.ShapeDtypeStruct((blocks, rows, pad), jnp.float32),
        in_specs=[hbm] * 9,
        out_specs=pl.BlockSpec(memory_space=pltpu.VMEM),
        scratch_shapes=[
            *[pltpu.SMEM(small.shape, small.dtype) for small in smalls],
            pltpu.SMEM((blocks,), jnp.int32),
            pltpu.SMEM((blocks,), jnp.int32),
            pltpu.VMEM((blocks, pad, pad), bf16),
            pltpu.VMEM((terms, sectors, pad, pad), bf16),
            pltpu.VMEM((owners, terms, sectors, pad, pad), bf16),
            *[pltpu.VMEM((sectors, pad, pad), bf16) for _ in range(terms)],
            pltpu.VMEM((blocks, pad, terms * pad), bf16),
            pltpu.VMEM((capacity, pad, pad), jnp.float32),
            pltpu.VMEM((term_devices, blocks, rows, pad), bf16),
            pltpu.VMEM((term_devices, blocks, rows, pad), bf16),
            pltpu.SemaphoreType.DMA((9,)),
            pltpu.SemaphoreType.DMA((2, owners - 1, terms)),
            pltpu.SemaphoreType.DMA((2, owners - 1, terms)),
            pltpu.SemaphoreType.DMA((groups, term_devices)),
            pltpu.SemaphoreType.DMA((groups, term_devices)),
        ],
        compiler_params=pltpu.CompilerParams(
            collective_id=0, has_side_effects=True, vmem_limit_bytes=40 * 1024 * 1024
        ),
        cost_estimate=pl.CostEstimate(
            flops=4 * blocks * terms * pad**3, bytes_accessed=4 * blocks * pad * pad, transcendentals=0
        ),
    )(*smalls, wavefunction, left_environment, right_environment)


def solution(mesh):
    return jax.shard_map(
        shards,
        mesh=mesh,
        in_specs=(
            P(("groups", "sector"), None, None),
            P(("groups", "term"), "sector"),
            P(("groups", "term"), "sector", None, None),
            P(("groups", "term"), "sector", None, None),
            P(("groups", "sector")),
            P(("groups", "sector")),
            P("groups"),
            P("groups"),
            P("groups"),
        ),
        out_specs=P(("groups", "sector"), "term", None),
        check_vma=False,
    )
```

```python
import functools

import jax
import jax.numpy as jnp
from jax import lax
from jax.experimental import pallas as pl
from jax.experimental.pallas import tpu as pltpu
from jax.sharding import PartitionSpec as P


def lookup(values_table, indices):
    matches = indices[:, None] == jnp.arange(values_table.shape[0])[None, :]
    return jnp.sum(jnp.where(matches, values_table[None, :], 0), axis=1)


def picked_shards(
    wavefunction,
    term_weights,
    left_environment,
    right_environment,
    left_sector,
    right_sector,
    right_place,
    left_dims,
    right_dims,
):
    block_count = wavefunction.shape[0]
    pad_size = wavefunction.shape[1]
    term_count = left_environment.shape[0]
    sector_count = left_environment.shape[1]
    owners = lax.axis_size("sector")
    own_index = lax.axis_index("sector")
    term_devices = lax.axis_size("term")
    capacity = max(2, 2 * block_count // owners)
    part_rows = pad_size // term_devices
    row_start = lax.axis_index("term") * part_rows
    columns = jnp.arange(pad_size)
    row_live = columns[None, :] < lookup(left_dims, left_sector)[:, None]
    col_live = columns[None, :] < lookup(right_dims, right_sector)[:, None]
    live_mask = row_live[:, :, None] & col_live[:, None, :]
    masked = jnp.where(live_mask, wavefunction, jnp.zeros_like(wavefunction))
    local_left = left_sector - own_index * sector_count
    env_rows = jnp.take(jnp.transpose(left_environment, (1, 0, 2, 3)), local_left, axis=0)
    left_part = jnp.einsum("bwij,bjk->bwik", env_rows, masked, preferred_element_type=jnp.float32)
    left_part = (left_part * jnp.transpose(term_weights)[:, :, None, None]).astype(jnp.bfloat16)
    storage = lookup(right_place, right_sector)
    target = storage // sector_count
    local_right = storage % sector_count
    right_by_slot = jnp.transpose(right_environment, (1, 0, 2, 3))
    all_place = lax.all_gather(storage, "sector", axis=0, tiled=True).reshape(owners, block_count)
    owned_here = all_place // sector_count == own_index
    sub_index = all_place % sector_count
    sector_ids = jnp.arange(sector_count)
    used_here = jnp.any(
        owned_here[:, :, None] & (sub_index[:, :, None] == sector_ids[None, None, :]), axis=1
    )
    reply_cap = min(capacity, sector_count)
    used_rank = jnp.cumsum(used_here.astype(jnp.int32), axis=1) - 1
    picked = used_here[:, None, :] & (used_rank[:, None, :] == jnp.arange(reply_cap)[None, :, None])
    chosen = jnp.sum(jnp.where(picked, sector_ids[None, None, :], 0), axis=2)
    valid_slot = jnp.any(picked, axis=2)
    outgoing = jnp.take(right_by_slot, chosen.reshape(-1), axis=0)
    outgoing = outgoing.reshape(owners, reply_cap, term_count, pad_size, pad_size)
    outgoing = jnp.where(valid_slot[:, :, None, None, None], outgoing, jnp.zeros_like(outgoing))
    incoming = lax.all_to_all(outgoing, "sector", split_axis=0, concat_axis=0, tiled=True)
    own_used = jnp.any(
        (target[:, None, None] == jnp.arange(owners)[None, :, None])
        & (local_right[:, None, None] == sector_ids[None, None, :]),
        axis=0,
    )
    own_rank = jnp.cumsum(own_used.astype(jnp.int32), axis=1) - 1
    reply_index = lookup(own_rank.reshape(-1), target * sector_count + local_right)
    env_cols = jnp.take(
        incoming.reshape(owners * reply_cap, term_count, pad_size, pad_size),
        target * reply_cap + reply_index,
        axis=0,
    )
    partial_value = jnp.einsum(
        "bwij,bwjk->bik", left_part, env_cols, preferred_element_type=jnp.float32
    ).astype(jnp.bfloat16)
    shares = lax.all_to_all(
        partial_value.reshape(block_count, term_devices, part_rows, pad_size),
        "term",
        split_axis=1,
        concat_axis=1,
        tiled=True,
    )
    result = jnp.sum(shares.astype(jnp.float32), axis=1)
    row_part = lax.dynamic_slice_in_dim(live_mask, row_start, part_rows, 1)
    return jnp.where(row_part, result, jnp.zeros_like(result))


MESH = pl.DeviceIdType.MESH


def chain_kernel(
    owners,
    term_devices,
    early,
    left_hbm,
    right_hbm,
    place_hbm,
    ldim_hbm,
    rdim_hbm,
    weight_hbm,
    theta_hbm,
    lenv_hbm,
    renv_hbm,
    out_ref,
    left_ref,
    right_ref,
    place_ref,
    ldim_ref,
    rdim_ref,
    weight_ref,
    perm_ref,
    inverse_ref,
    theta,
    lenv,
    near,
    *rest,
):
    terms, sectors, pad = renv_hbm.shape[0], renv_hbm.shape[1], renv_hbm.shape[2]
    far = rest[:terms]
    (part, total, give, take, local_sem, gather_send, gather_recv, share_send, share_recv) = rest[terms:]
    blocks = theta_hbm.shape[0]
    late = blocks - early
    rows = pad // term_devices
    me = lax.axis_index("sector")
    mine = lax.axis_index("term")

    def last_of(device):
        return (owners - 1) * (1 - (2 * device) // owners)

    barrier = pltpu.get_barrier_semaphore()
    for step in (-1, 1):
        @pl.when((me + step >= 0) & (me + step < owners))
        def _():
            pl.semaphore_signal(barrier, inc=1, device_id={"sector": me + step}, device_id_type=MESH)
    for step in range(1, term_devices):
        pl.semaphore_signal(
            barrier, inc=1, device_id={"term": (mine + step) % term_devices}, device_id_type=MESH
        )
    neighbours = (me + owners - 1) // owners + (2 * owners - 2 - me) // owners
    pl.semaphore_wait(barrier, term_devices - 1 + neighbours)

    def hop(src, dst, way, distance, term, step):
        return pltpu.make_async_remote_copy(
            src_ref=src,
            dst_ref=dst,
            send_sem=gather_send.at[way, distance, term],
            recv_sem=gather_recv.at[way, distance, term],
            device_id={"sector": me + step},
            device_id_type=MESH,
        )

    def pass_on(src, owner, way, distance, term, step):
        target = me + step

        @pl.when((target >= 0) & (target < owners) & (owner != last_of(target)))
        def _():
            hop(src, near.at[owner, term], way, distance, term, step).start()

        @pl.when((target >= 0) & (target < owners) & (owner == last_of(target)))
        def _():
            hop(src, far[term], way, distance, term, step).start()

    for term in range(terms):
        for way, step in ((0, 1), (1, -1)):
            pass_on(renv_hbm.at[term], me, way, 0, term, step)
    copies = [
        pltpu.make_async_copy(src, dst, local_sem.at[index])
        for index, (src, dst) in enumerate((
            (left_hbm, left_ref),
            (right_hbm, right_ref),
            (place_hbm, place_ref),
            (ldim_hbm, ldim_ref),
            (rdim_hbm, rdim_ref),
            (weight_hbm, weight_ref),
            (theta_hbm, theta),
            (lenv_hbm, lenv),
            (renv_hbm, near.at[me]),
        ))
    ]
    for copy in copies:
        copy.start()
    for copy in copies:
        copy.wait()

    row_ids = lax.broadcasted_iota(jnp.int32, (pad, pad), 0)
    col_ids = lax.broadcasted_iota(jnp.int32, (pad, pad), 1)

    def left_product(block):
        sector = left_ref[block]
        live = (row_ids < ldim_ref[sector]) & (col_ids < rdim_ref[right_ref[block]])
        state = jnp.where(live, theta[block].astype(jnp.float32), 0.0).astype(jnp.bfloat16)
        local = sector % sectors
        stack = jnp.concatenate([lenv[term, local] for term in range(terms)], axis=0)
        product = jnp.dot(stack, state, preferred_element_type=jnp.float32)
        for term in range(terms):
            scaled = product[term * pad:(term + 1) * pad] * weight_ref[term, block]
            part[block, :, term * pad:(term + 1) * pad] = scaled.astype(jnp.bfloat16)

    unroll = 2 if early % 2 == 0 and late % 2 == 0 else 1

    def each(count, body, first=0):
        def step(index, carry):
            for inner in range(unroll):
                body(first + index * unroll + inner)
            return carry
        lax.fori_loop(0, count // unroll, step, 0)

    each(blocks, left_product)

    def is_late(block):
        return (place_ref[right_ref[block]] // sectors == last_of(me)).astype(jnp.int32)

    late_total = lax.fori_loop(0, blocks, lambda block, count: count + is_late(block), 0)

    def rank(block, late_before):
        flag = is_late(block)
        inverse_ref[block] = jnp.where(
            flag == 1, blocks - late_total + late_before, block - late_before
        )
        return late_before + flag

    lax.fori_loop(0, blocks, rank, 0)

    def invert(slot, carry):
        found = 0
        for block in range(blocks):
            found += jnp.where(inverse_ref[block] == slot, block, 0)
        perm_ref[slot] = found
        return carry

    lax.fori_loop(0, blocks, invert, 0)

    def arrive(distance, term):
        for way, step in ((0, 1), (1, -1)):
            owner = me - step * distance
            @pl.when((owner >= 0) & (owner < owners) & (owner != last_of(me)))
            def _():
                hop(near.at[me, term], near.at[owner, term], way, distance - 1, term, step).wait_recv()
                if distance < owners - 1:
                    pass_on(near.at[owner, term], owner, way, distance, term, step)

    def arrive_far(distance, term):
        for way, step in ((0, 1), (1, -1)):
            owner = me - step * distance
            @pl.when((owner >= 0) & (owner < owners) & (owner == last_of(me)))
            def _():
                hop(near.at[me, term], far[term], way, distance - 1, term, step).wait_recv()
                if distance < owners - 1:
                    pass_on(far[term], owner, way, distance, term, step)

    for distance in range(1, owners - 1):
        for term in range(terms):
            arrive(distance, term)
            if distance < owners - 1:
                arrive_far(distance, term)

    def near_product(slot):
        block = perm_ref[slot]
        storage = place_ref[right_ref[block]]
        owner = storage // sectors
        sub = storage % sectors
        owner = jnp.where(owner == last_of(me), me, owner)
        stack = jnp.concatenate([near[owner, term, sub] for term in range(terms)], axis=0)
        return jnp.dot(part[block], stack, preferred_element_type=jnp.float32)

    def put(slot, value):
        rounded = value.astype(jnp.bfloat16)
        for device in range(term_devices):
            give[device, slot] = rounded[device * rows:(device + 1) * rows]

    def share(first, count, group, peer):
        other = (mine + peer) % term_devices
        return pltpu.make_async_remote_copy(
            src_ref=give.at[other, pl.ds(first, count)],
            dst_ref=take.at[peer, pl.ds(first, count)],
            send_sem=share_send.at[group, peer],
            recv_sem=share_recv.at[group, peer],
            device_id={"term": other},
            device_id_type=MESH,
        )

    def pieces(first, count):
        cut = 3 if count % 6 == 0 else 1
        return [(first + i * (count // cut), count // cut) for i in range(cut)]

    groups = pieces(0, early) + pieces(early, late)
    early_groups = len(pieces(0, early))

    for group in range(early_groups):
        first, count = groups[group]
        each(count, lambda slot: put(slot, near_product(slot)), first)
        for peer in range(1, term_devices):
            share(first, count, group, peer).start()

    def keep(slot):
        total[slot - early] = near_product(slot)

    each(late, keep, early)

    def far_product(slot, term):
        block = perm_ref[slot]
        storage = place_ref[right_ref[block]]
        here = storage // sectors == last_of(me)
        sub = storage % sectors
        value = jnp.dot(
            part[block, :, term * pad:(term + 1) * pad], far[term][sub], preferred_element_type=jnp.float32
        )
        held = total[slot - early]
        added = value if term == 0 else held + value
        return jnp.where(here, added, held)

    for term in range(terms):
        arrive_far(owners - 1, term)
        if term < terms - 1:
            def add(slot, term=term):
                total[slot - early] = far_product(slot, term)
            each(late, add, early)
    for group in range(early_groups, len(groups)):
        first, count = groups[group]
        each(count, lambda slot: put(slot, far_product(slot, terms - 1)), first)
        for peer in range(1, term_devices):
            share(first, count, group, peer).start()

    for group, (first, count) in enumerate(groups):
        for peer in range(1, term_devices):
            share(first, count, group, peer).wait_recv()

    out_rows = lax.broadcasted_iota(jnp.int32, (rows, pad), 0) + mine * rows
    out_cols = lax.broadcasted_iota(jnp.int32, (rows, pad), 1)

    def finish(block):
        slot = inverse_ref[block]
        value = give[mine, slot].astype(jnp.float32)
        for peer in range(1, term_devices):
            value = value + take[peer, slot].astype(jnp.float32)
        live = (out_rows < ldim_ref[left_ref[block]]) & (out_cols < rdim_ref[right_ref[block]])
        out_ref[block] = jnp.where(live, value, 0.0)

    each(blocks, finish)

    for group, (first, count) in enumerate(groups):
        for peer in range(1, term_devices):
            share(first, count, group, peer).wait_send()
    for distance in range(owners - 1):
        for term in range(terms):
            for way, step in ((0, 1), (1, -1)):
                origin = me - step * distance
                @pl.when((origin >= 0) & (origin < owners) & (me + step >= 0) & (me + step < owners))
                def _():
                    hop(near.at[me, term], near.at[me, term], way, distance, term, step).wait_send()


def shards(
    wavefunction,
    term_weights,
    left_environment,
    right_environment,
    left_sector,
    right_sector,
    right_place,
    left_dims,
    right_dims,
):
    blocks, pad, _ = wavefunction.shape
    terms, sectors = left_environment.shape[:2]
    owners = lax.axis_size("sector")
    term_devices = lax.axis_size("term")
    capacity = max(2, 2 * blocks // owners)
    if capacity < sectors or owners < 3:
        return picked_shards(
            wavefunction,
            term_weights,
            left_environment,
            right_environment,
            left_sector,
            right_sector,
            right_place,
            left_dims,
            right_dims,
        )
    early = blocks - capacity
    rows = pad // term_devices
    hbm = pl.BlockSpec(memory_space=pltpu.HBM)
    smalls = (left_sector, right_sector, right_place, left_dims, right_dims, term_weights)
    bf16 = jnp.bfloat16
    groups = (3 if early % 6 == 0 else 1) + (3 if capacity % 6 == 0 else 1)
    return pl.pallas_call(
        functools.partial(chain_kernel, owners, term_devices, early),
        out_shape=jax.ShapeDtypeStruct((blocks, rows, pad), jnp.float32),
        in_specs=[hbm] * 9,
        out_specs=pl.BlockSpec(memory_space=pltpu.VMEM),
        scratch_shapes=[
            *[pltpu.SMEM(small.shape, small.dtype) for small in smalls],
            pltpu.SMEM((blocks,), jnp.int32),
            pltpu.SMEM((blocks,), jnp.int32),
            pltpu.VMEM((blocks, pad, pad), bf16),
            pltpu.VMEM((terms, sectors, pad, pad), bf16),
            pltpu.VMEM((owners, terms, sectors, pad, pad), bf16),
            *[pltpu.VMEM((sectors, pad, pad), bf16) for _ in range(terms)],
            pltpu.VMEM((blocks, pad, terms * pad), bf16),
            pltpu.VMEM((capacity, pad, pad), jnp.float32),
            pltpu.VMEM((term_devices, blocks, rows, pad), bf16),
            pltpu.VMEM((term_devices, blocks, rows, pad), bf16),
            pltpu.SemaphoreType.DMA((9,)),
            pltpu.SemaphoreType.DMA((2, owners - 1, terms)),
            pltpu.SemaphoreType.DMA((2, owners - 1, terms)),
            pltpu.SemaphoreType.DMA((groups, term_devices)),
            pltpu.SemaphoreType.DMA((groups, term_devices)),
        ],
        compiler_params=pltpu.CompilerParams(
            collective_id=0, has_side_effects=True, vmem_limit_bytes=56 * 1024 * 1024
        ),
        cost_estimate=pl.CostEstimate(
            flops=4 * blocks * terms * pad**3, bytes_accessed=4 * blocks * pad * pad, transcendentals=0
        ),
    )(*smalls, wavefunction, left_environment, right_environment)


def solution(mesh):
    return jax.shard_map(
        shards,
        mesh=mesh,
        in_specs=(
            P(("groups", "sector"), None, None),
            P(("groups", "term"), "sector"),
            P(("groups", "term"), "sector", None, None),
            P(("groups", "term"), "sector", None, None),
            P(("groups", "sector")),
            P(("groups", "sector")),
            P("groups"),
            P("groups"),
            P("groups"),
        ),
        out_specs=P(("groups", "sector"), "term", None),
        check_vma=False,
    )
```

```python
import functools

import jax
import jax.numpy as jnp
from jax import lax
from jax.experimental import pallas as pl
from jax.experimental.pallas import tpu as pltpu
from jax.sharding import PartitionSpec as P


def lookup(values_table, indices):
    matches = indices[:, None] == jnp.arange(values_table.shape[0])[None, :]
    return jnp.sum(jnp.where(matches, values_table[None, :], 0), axis=1)


def picked_shards(
    wavefunction,
    term_weights,
    left_environment,
    right_environment,
    left_sector,
    right_sector,
    right_place,
    left_dims,
    right_dims,
):
    block_count = wavefunction.shape[0]
    pad_size = wavefunction.shape[1]
    term_count = left_environment.shape[0]
    sector_count = left_environment.shape[1]
    owners = lax.axis_size("sector")
    own_index = lax.axis_index("sector")
    term_devices = lax.axis_size("term")
    capacity = max(2, 2 * block_count // owners)
    part_rows = pad_size // term_devices
    row_start = lax.axis_index("term") * part_rows
    columns = jnp.arange(pad_size)
    row_live = columns[None, :] < lookup(left_dims, left_sector)[:, None]
    col_live = columns[None, :] < lookup(right_dims, right_sector)[:, None]
    live_mask = row_live[:, :, None] & col_live[:, None, :]
    masked = jnp.where(live_mask, wavefunction, jnp.zeros_like(wavefunction))
    local_left = left_sector - own_index * sector_count
    env_rows = jnp.take(jnp.transpose(left_environment, (1, 0, 2, 3)), local_left, axis=0)
    left_part = jnp.einsum("bwij,bjk->bwik", env_rows, masked, preferred_element_type=jnp.float32)
    left_part = (left_part * jnp.transpose(term_weights)[:, :, None, None]).astype(jnp.bfloat16)
    storage = lookup(right_place, right_sector)
    target = storage // sector_count
    local_right = storage % sector_count
    right_by_slot = jnp.transpose(right_environment, (1, 0, 2, 3))
    all_place = lax.all_gather(storage, "sector", axis=0, tiled=True).reshape(owners, block_count)
    owned_here = all_place // sector_count == own_index
    sub_index = all_place % sector_count
    sector_ids = jnp.arange(sector_count)
    used_here = jnp.any(
        owned_here[:, :, None] & (sub_index[:, :, None] == sector_ids[None, None, :]), axis=1
    )
    reply_cap = min(capacity, sector_count)
    used_rank = jnp.cumsum(used_here.astype(jnp.int32), axis=1) - 1
    picked = used_here[:, None, :] & (used_rank[:, None, :] == jnp.arange(reply_cap)[None, :, None])
    chosen = jnp.sum(jnp.where(picked, sector_ids[None, None, :], 0), axis=2)
    valid_slot = jnp.any(picked, axis=2)
    outgoing = jnp.take(right_by_slot, chosen.reshape(-1), axis=0)
    outgoing = outgoing.reshape(owners, reply_cap, term_count, pad_size, pad_size)
    outgoing = jnp.where(valid_slot[:, :, None, None, None], outgoing, jnp.zeros_like(outgoing))
    incoming = lax.all_to_all(outgoing, "sector", split_axis=0, concat_axis=0, tiled=True)
    own_used = jnp.any(
        (target[:, None, None] == jnp.arange(owners)[None, :, None])
        & (local_right[:, None, None] == sector_ids[None, None, :]),
        axis=0,
    )
    own_rank = jnp.cumsum(own_used.astype(jnp.int32), axis=1) - 1
    reply_index = lookup(own_rank.reshape(-1), target * sector_count + local_right)
    env_cols = jnp.take(
        incoming.reshape(owners * reply_cap, term_count, pad_size, pad_size),
        target * reply_cap + reply_index,
        axis=0,
    )
    partial_value = jnp.einsum(
        "bwij,bwjk->bik", left_part, env_cols, preferred_element_type=jnp.float32
    ).astype(jnp.bfloat16)
    shares = lax.all_to_all(
        partial_value.reshape(block_count, term_devices, part_rows, pad_size),
        "term",
        split_axis=1,
        concat_axis=1,
        tiled=True,
    )
    result = jnp.sum(shares.astype(jnp.float32), axis=1)
    row_part = lax.dynamic_slice_in_dim(live_mask, row_start, part_rows, 1)
    return jnp.where(row_part, result, jnp.zeros_like(result))


MESH = pl.DeviceIdType.MESH


def chain_kernel(
    owners,
    term_devices,
    early,
    left_hbm,
    right_hbm,
    place_hbm,
    ldim_hbm,
    rdim_hbm,
    weight_hbm,
    theta_hbm,
    lenv_hbm,
    renv_hbm,
    out_ref,
    left_ref,
    right_ref,
    place_ref,
    ldim_ref,
    rdim_ref,
    weight_ref,
    perm_ref,
    inverse_ref,
    theta,
    lenv,
    near,
    *rest,
):
    terms, sectors, pad = renv_hbm.shape[0], renv_hbm.shape[1], renv_hbm.shape[2]
    far = rest[:terms]
    (part, total, own, take, local_sem, gather_send, gather_recv, share_send, share_recv) = rest[terms:terms + 9]
    buffers = rest[terms + 9:]
    give, pair, mid = buffers[0::3], buffers[1::3], buffers[2::3]
    blocks = theta_hbm.shape[0]
    late = blocks - early
    rows = pad // term_devices
    me = lax.axis_index("sector")
    mine = lax.axis_index("term")

    def last_of(device):
        return (owners - 1) * (1 - (2 * device) // owners)

    barrier = pltpu.get_barrier_semaphore()
    for step in (-1, 1):
        @pl.when((me + step >= 0) & (me + step < owners))
        def _():
            pl.semaphore_signal(barrier, inc=1, device_id={"sector": me + step}, device_id_type=MESH)
    peers = [mine // 2 * 2 + 1 - mine % 2] + [(mine + 2 * i) % term_devices for i in range(1, term_devices // 2)]
    for peer in peers:
        pl.semaphore_signal(barrier, inc=1, device_id={"term": peer}, device_id_type=MESH)
    neighbours = (me + owners - 1) // owners + (2 * owners - 2 - me) // owners
    pl.semaphore_wait(barrier, len(peers) + neighbours)

    def hop(src, dst, way, distance, term, step):
        return pltpu.make_async_remote_copy(
            src_ref=src,
            dst_ref=dst,
            send_sem=gather_send.at[way, distance, term],
            recv_sem=gather_recv.at[way, distance, term],
            device_id={"sector": me + step},
            device_id_type=MESH,
        )

    def pass_on(src, owner, way, distance, term, step):
        target = me + step

        @pl.when((target >= 0) & (target < owners) & (owner != last_of(target)))
        def _():
            hop(src, near.at[owner, term], way, distance, term, step).start()

        @pl.when((target >= 0) & (target < owners) & (owner == last_of(target)))
        def _():
            hop(src, far[term], way, distance, term, step).start()

    for term in range(terms):
        for way, step in ((0, 1), (1, -1)):
            pass_on(renv_hbm.at[term], me, way, 0, term, step)
    copies = [
        pltpu.make_async_copy(src, dst, local_sem.at[index])
        for index, (src, dst) in enumerate((
            (left_hbm, left_ref),
            (right_hbm, right_ref),
            (place_hbm, place_ref),
            (ldim_hbm, ldim_ref),
            (rdim_hbm, rdim_ref),
            (weight_hbm, weight_ref),
            (theta_hbm, theta),
            (lenv_hbm, lenv),
            (renv_hbm, near.at[me]),
        ))
    ]
    for copy in copies:
        copy.start()
    for copy in copies:
        copy.wait()

    row_ids = lax.broadcasted_iota(jnp.int32, (pad, pad), 0)
    col_ids = lax.broadcasted_iota(jnp.int32, (pad, pad), 1)

    def left_product(block):
        sector = left_ref[block]
        live = (row_ids < ldim_ref[sector]) & (col_ids < rdim_ref[right_ref[block]])
        state = jnp.where(live, theta[block].astype(jnp.float32), 0.0).astype(jnp.bfloat16)
        local = sector % sectors
        stack = jnp.concatenate([lenv[term, local] for term in range(terms)], axis=0)
        product = jnp.dot(stack, state, preferred_element_type=jnp.float32)
        for term in range(terms):
            scaled = product[term * pad:(term + 1) * pad] * weight_ref[term, block]
            part[block, :, term * pad:(term + 1) * pad] = scaled.astype(jnp.bfloat16)

    unroll = 2 if early % 2 == 0 and late % 2 == 0 else 1

    def each(count, body, first=0):
        def step(index, carry):
            for inner in range(unroll):
                body(first + index * unroll + inner)
            return carry
        lax.fori_loop(0, count // unroll, step, 0)

    each(blocks, left_product)

    def is_late(block):
        return (place_ref[right_ref[block]] // sectors == last_of(me)).astype(jnp.int32)

    late_total = lax.fori_loop(0, blocks, lambda block, count: count + is_late(block), 0)

    def rank(block, late_before):
        flag = is_late(block)
        inverse_ref[block] = jnp.where(
            flag == 1, blocks - late_total + late_before, block - late_before
        )
        return late_before + flag

    lax.fori_loop(0, blocks, rank, 0)

    def invert(slot, carry):
        found = 0
        for block in range(blocks):
            found += jnp.where(inverse_ref[block] == slot, block, 0)
        perm_ref[slot] = found
        return carry

    lax.fori_loop(0, blocks, invert, 0)

    def arrive(distance, term):
        for way, step in ((0, 1), (1, -1)):
            owner = me - step * distance
            @pl.when((owner >= 0) & (owner < owners) & (owner != last_of(me)))
            def _():
                hop(near.at[me, term], near.at[owner, term], way, distance - 1, term, step).wait_recv()
                if distance < owners - 1:
                    pass_on(near.at[owner, term], owner, way, distance, term, step)

    def arrive_far(distance, term):
        for way, step in ((0, 1), (1, -1)):
            owner = me - step * distance
            @pl.when((owner >= 0) & (owner < owners) & (owner == last_of(me)))
            def _():
                hop(near.at[me, term], far[term], way, distance - 1, term, step).wait_recv()
                if distance < owners - 1:
                    pass_on(far[term], owner, way, distance, term, step)

    for distance in range(1, owners - 1):
        for term in range(terms):
            arrive(distance, term)
            if distance < owners - 1:
                arrive_far(distance, term)

    def near_product(slot):
        block = perm_ref[slot]
        storage = place_ref[right_ref[block]]
        owner = storage // sectors
        sub = storage % sectors
        owner = jnp.where(owner == last_of(me), me, owner)
        stack = jnp.concatenate([near[owner, term, sub] for term in range(terms)], axis=0)
        return jnp.dot(part[block], stack, preferred_element_type=jnp.float32)

    halves = term_devices // 2
    far_half, core = mine // 2, mine % 2

    def put(group, slot, value):
        rounded = value.astype(jnp.bfloat16)
        for device in range(term_devices):
            give[group][device % 2, slot - groups[group][0], device // 2] = rounded[device * rows:(device + 1) * rows]

    def swap(first, count, group):
        return pltpu.make_async_remote_copy(
            src_ref=give[group].at[1 - core],
            dst_ref=pair[group],
            send_sem=share_send.at[group, 0],
            recv_sem=share_recv.at[group, 0],
            device_id={"term": far_half * 2 + 1 - core},
            device_id_type=MESH,
        )

    def share(first, count, group, peer):
        return pltpu.make_async_remote_copy(
            src_ref=mid[group].at[peer],
            dst_ref=take.at[peer, pl.ds(first, count)],
            send_sem=share_send.at[group, peer],
            recv_sem=share_recv.at[group, peer],
            device_id={"term": (far_half + peer) % halves * 2 + core},
            device_id_type=MESH,
        )

    def cross(group):
        first, count = groups[group]
        swap(first, count, group).wait_recv()
        for peer in range(halves):
            other = (far_half + peer) % halves
            value = give[group][core, :, other].astype(jnp.float32) + pair[group][:, other].astype(jnp.float32)
            if peer:
                mid[group][peer] = value.astype(jnp.bfloat16)
                share(first, count, group, peer).start()
            else:
                own[pl.ds(first, count)] = value

    def pieces(first, count):
        cut = 3 if count % 6 == 0 else 1
        return [(first + i * (count // cut), count // cut) for i in range(cut)]

    groups = pieces(0, early) + pieces(early, late)
    early_groups = len(pieces(0, early))

    for group in range(early_groups):
        first, count = groups[group]
        each(count, lambda slot: put(group, slot, near_product(slot)), first)
        swap(first, count, group).start()

    def keep(slot):
        total[slot - early] = near_product(slot)

    each(late, keep, early)
    for group in range(early_groups):
        cross(group)

    def far_product(slot, term):
        block = perm_ref[slot]
        storage = place_ref[right_ref[block]]
        here = storage // sectors == last_of(me)
        sub = storage % sectors
        value = jnp.dot(
            part[block, :, term * pad:(term + 1) * pad], far[term][sub], preferred_element_type=jnp.float32
        )
        held = total[slot - early]
        added = value if term == 0 else held + value
        return jnp.where(here, added, held)

    for term in range(terms):
        arrive_far(owners - 1, term)
        if term < terms - 1:
            def add(slot, term=term):
                total[slot - early] = far_product(slot, term)
            each(late, add, early)
    for group in range(early_groups, len(groups)):
        first, count = groups[group]
        each(count, lambda slot: put(group, slot, far_product(slot, terms - 1)), first)
        swap(first, count, group).start()
        if group > early_groups:
            cross(group - 1)
    cross(len(groups) - 1)

    for group, (first, count) in enumerate(groups):
        for peer in range(1, halves):
            share(first, count, group, peer).wait_recv()

    out_rows = lax.broadcasted_iota(jnp.int32, (rows, pad), 0) + mine * rows
    out_cols = lax.broadcasted_iota(jnp.int32, (rows, pad), 1)

    def finish(block):
        slot = inverse_ref[block]
        value = own[slot]
        for peer in range(1, halves):
            value = value + take[peer, slot].astype(jnp.float32)
        live = (out_rows < ldim_ref[left_ref[block]]) & (out_cols < rdim_ref[right_ref[block]])
        out_ref[block] = jnp.where(live, value, 0.0)

    each(blocks, finish)

    for group, (first, count) in enumerate(groups):
        swap(first, count, group).wait_send()
        for peer in range(1, halves):
            share(first, count, group, peer).wait_send()
    for distance in range(owners - 1):
        for term in range(terms):
            for way, step in ((0, 1), (1, -1)):
                origin = me - step * distance
                @pl.when((origin >= 0) & (origin < owners) & (me + step >= 0) & (me + step < owners))
                def _():
                    hop(near.at[me, term], near.at[me, term], way, distance, term, step).wait_send()


def shards(
    wavefunction,
    term_weights,
    left_environment,
    right_environment,
    left_sector,
    right_sector,
    right_place,
    left_dims,
    right_dims,
):
    blocks, pad, _ = wavefunction.shape
    terms, sectors = left_environment.shape[:2]
    owners = lax.axis_size("sector")
    term_devices = lax.axis_size("term")
    capacity = max(2, 2 * blocks // owners)
    if capacity < sectors or owners < 3 or term_devices % 2:
        return picked_shards(
            wavefunction,
            term_weights,
            left_environment,
            right_environment,
            left_sector,
            right_sector,
            right_place,
            left_dims,
            right_dims,
        )
    early = blocks - capacity
    rows = pad // term_devices
    hbm = pl.BlockSpec(memory_space=pltpu.HBM)
    smalls = (left_sector, right_sector, right_place, left_dims, right_dims, term_weights)
    bf16 = jnp.bfloat16
    counts = [n // cut for n in (early, capacity) for cut in (3 if n % 6 == 0 else 1,) for _ in range(cut)]
    groups = len(counts)
    return pl.pallas_call(
        functools.partial(chain_kernel, owners, term_devices, early),
        out_shape=jax.ShapeDtypeStruct((blocks, rows, pad), jnp.float32),
        in_specs=[hbm] * 9,
        out_specs=pl.BlockSpec(memory_space=pltpu.VMEM),
        scratch_shapes=[
            *[pltpu.SMEM(small.shape, small.dtype) for small in smalls],
            pltpu.SMEM((blocks,), jnp.int32),
            pltpu.SMEM((blocks,), jnp.int32),
            pltpu.VMEM((blocks, pad, pad), bf16),
            pltpu.VMEM((terms, sectors, pad, pad), bf16),
            pltpu.VMEM((owners, terms, sectors, pad, pad), bf16),
            *[pltpu.VMEM((sectors, pad, pad), bf16) for _ in range(terms)],
            pltpu.VMEM((blocks, pad, terms * pad), bf16),
            pltpu.VMEM((capacity, pad, pad), jnp.float32),
            pltpu.VMEM((blocks, rows, pad), jnp.float32),
            pltpu.VMEM((term_devices // 2, blocks, rows, pad), bf16),
            pltpu.SemaphoreType.DMA((9,)),
            pltpu.SemaphoreType.DMA((2, owners - 1, terms)),
            pltpu.SemaphoreType.DMA((2, owners - 1, terms)),
            pltpu.SemaphoreType.DMA((groups, term_devices // 2)),
            pltpu.SemaphoreType.DMA((groups, term_devices // 2)),
            *[
                pltpu.VMEM(shape, bf16)
                for count in counts
                for shape in (
                    (2, count, term_devices // 2, rows, pad),
                    (count, term_devices // 2, rows, pad),
                    (term_devices // 2, count, rows, pad),
                )
            ],
        ],
        compiler_params=pltpu.CompilerParams(
            collective_id=0, has_side_effects=True, vmem_limit_bytes=56 * 1024 * 1024
        ),
        cost_estimate=pl.CostEstimate(
            flops=4 * blocks * terms * pad**3, bytes_accessed=4 * blocks * pad * pad, transcendentals=0
        ),
    )(*smalls, wavefunction, left_environment, right_environment)


def solution(mesh):
    return jax.shard_map(
        shards,
        mesh=mesh,
        in_specs=(
            P(("groups", "sector"), None, None),
            P(("groups", "term"), "sector"),
            P(("groups", "term"), "sector", None, None),
            P(("groups", "term"), "sector", None, None),
            P(("groups", "sector")),
            P(("groups", "sector")),
            P("groups"),
            P("groups"),
            P("groups"),
        ),
        out_specs=P(("groups", "sector"), "term", None),
        check_vma=False,
    )
```

```python
import functools

import jax
import jax.numpy as jnp
from jax import lax
from jax.experimental import pallas as pl
from jax.experimental.pallas import tpu as pltpu
from jax.sharding import PartitionSpec as P


def lookup(values_table, indices):
    matches = indices[:, None] == jnp.arange(values_table.shape[0])[None, :]
    return jnp.sum(jnp.where(matches, values_table[None, :], 0), axis=1)


def picked_shards(
    wavefunction,
    term_weights,
    left_environment,
    right_environment,
    left_sector,
    right_sector,
    right_place,
    left_dims,
    right_dims,
):
    block_count = wavefunction.shape[0]
    pad_size = wavefunction.shape[1]
    term_count = left_environment.shape[0]
    sector_count = left_environment.shape[1]
    owners = lax.axis_size("sector")
    own_index = lax.axis_index("sector")
    term_devices = lax.axis_size("term")
    capacity = max(2, 2 * block_count // owners)
    part_rows = pad_size // term_devices
    row_start = lax.axis_index("term") * part_rows
    columns = jnp.arange(pad_size)
    row_live = columns[None, :] < lookup(left_dims, left_sector)[:, None]
    col_live = columns[None, :] < lookup(right_dims, right_sector)[:, None]
    live_mask = row_live[:, :, None] & col_live[:, None, :]
    masked = jnp.where(live_mask, wavefunction, jnp.zeros_like(wavefunction))
    local_left = left_sector - own_index * sector_count
    env_rows = jnp.take(jnp.transpose(left_environment, (1, 0, 2, 3)), local_left, axis=0)
    left_part = jnp.einsum("bwij,bjk->bwik", env_rows, masked, preferred_element_type=jnp.float32)
    left_part = (left_part * jnp.transpose(term_weights)[:, :, None, None]).astype(jnp.bfloat16)
    storage = lookup(right_place, right_sector)
    target = storage // sector_count
    local_right = storage % sector_count
    right_by_slot = jnp.transpose(right_environment, (1, 0, 2, 3))
    all_place = lax.all_gather(storage, "sector", axis=0, tiled=True).reshape(owners, block_count)
    owned_here = all_place // sector_count == own_index
    sub_index = all_place % sector_count
    sector_ids = jnp.arange(sector_count)
    used_here = jnp.any(
        owned_here[:, :, None] & (sub_index[:, :, None] == sector_ids[None, None, :]), axis=1
    )
    reply_cap = min(capacity, sector_count)
    used_rank = jnp.cumsum(used_here.astype(jnp.int32), axis=1) - 1
    picked = used_here[:, None, :] & (used_rank[:, None, :] == jnp.arange(reply_cap)[None, :, None])
    chosen = jnp.sum(jnp.where(picked, sector_ids[None, None, :], 0), axis=2)
    valid_slot = jnp.any(picked, axis=2)
    outgoing = jnp.take(right_by_slot, chosen.reshape(-1), axis=0)
    outgoing = outgoing.reshape(owners, reply_cap, term_count, pad_size, pad_size)
    outgoing = jnp.where(valid_slot[:, :, None, None, None], outgoing, jnp.zeros_like(outgoing))
    incoming = lax.all_to_all(outgoing, "sector", split_axis=0, concat_axis=0, tiled=True)
    own_used = jnp.any(
        (target[:, None, None] == jnp.arange(owners)[None, :, None])
        & (local_right[:, None, None] == sector_ids[None, None, :]),
        axis=0,
    )
    own_rank = jnp.cumsum(own_used.astype(jnp.int32), axis=1) - 1
    reply_index = lookup(own_rank.reshape(-1), target * sector_count + local_right)
    env_cols = jnp.take(
        incoming.reshape(owners * reply_cap, term_count, pad_size, pad_size),
        target * reply_cap + reply_index,
        axis=0,
    )
    partial_value = jnp.einsum(
        "bwij,bwjk->bik", left_part, env_cols, preferred_element_type=jnp.float32
    ).astype(jnp.bfloat16)
    shares = lax.all_to_all(
        partial_value.reshape(block_count, term_devices, part_rows, pad_size),
        "term",
        split_axis=1,
        concat_axis=1,
        tiled=True,
    )
    result = jnp.sum(shares.astype(jnp.float32), axis=1)
    row_part = lax.dynamic_slice_in_dim(live_mask, row_start, part_rows, 1)
    return jnp.where(row_part, result, jnp.zeros_like(result))


MESH = pl.DeviceIdType.MESH


def chain_kernel(
    owners,
    term_devices,
    early,
    left_hbm,
    right_hbm,
    place_hbm,
    ldim_hbm,
    rdim_hbm,
    weight_hbm,
    theta_hbm,
    lenv_hbm,
    renv_hbm,
    out_ref,
    left_ref,
    right_ref,
    place_ref,
    ldim_ref,
    rdim_ref,
    weight_ref,
    perm_ref,
    inverse_ref,
    theta,
    lenv,
    near,
    *rest,
):
    terms, sectors, pad = renv_hbm.shape[0], renv_hbm.shape[1], renv_hbm.shape[2]
    far = rest[:terms]
    (part, total, own, take, local_sem, gather_send, gather_recv, share_send, share_recv) = rest[terms:terms + 9]
    buffers = rest[terms + 9:]
    give, pair, mid = buffers[0::3], buffers[1::3], buffers[2::3]
    blocks = theta_hbm.shape[0]
    late = blocks - early
    rows = pad // term_devices
    me = lax.axis_index("sector")
    mine = lax.axis_index("term")

    def last_of(device):
        return (owners - 1) * (1 - (2 * device) // owners)

    barrier = pltpu.get_barrier_semaphore()
    for step in (-1, 1):
        @pl.when((me + step >= 0) & (me + step < owners))
        def _():
            pl.semaphore_signal(barrier, inc=1, device_id={"sector": me + step}, device_id_type=MESH)
    peers = [mine // 2 * 2 + 1 - mine % 2] + [(mine + 2 * i) % term_devices for i in range(1, term_devices // 2)]
    for peer in peers:
        pl.semaphore_signal(barrier, inc=1, device_id={"term": peer}, device_id_type=MESH)
    neighbours = (me + owners - 1) // owners + (2 * owners - 2 - me) // owners
    pl.semaphore_wait(barrier, len(peers) + neighbours)

    def hop(src, dst, way, distance, term, step):
        return pltpu.make_async_remote_copy(
            src_ref=src,
            dst_ref=dst,
            send_sem=gather_send.at[way, distance, term],
            recv_sem=gather_recv.at[way, distance, term],
            device_id={"sector": me + step},
            device_id_type=MESH,
        )

    def pass_on(src, owner, way, distance, term, step):
        target = me + step

        @pl.when((target >= 0) & (target < owners) & (owner != last_of(target)))
        def _():
            hop(src, near.at[owner, term], way, distance, term, step).start()

        @pl.when((target >= 0) & (target < owners) & (owner == last_of(target)))
        def _():
            hop(src, far[term], way, distance, term, step).start()

    for term in range(terms):
        for way, step in ((0, 1), (1, -1)):
            pass_on(renv_hbm.at[term], me, way, 0, term, step)
    copies = [
        pltpu.make_async_copy(src, dst, local_sem.at[index])
        for index, (src, dst) in enumerate((
            (left_hbm, left_ref),
            (right_hbm, right_ref),
            (place_hbm, place_ref),
            (ldim_hbm, ldim_ref),
            (rdim_hbm, rdim_ref),
            (weight_hbm, weight_ref),
            (theta_hbm, theta),
            (lenv_hbm, lenv),
            (renv_hbm, near.at[me]),
        ))
    ]
    for copy in copies:
        copy.start()
    for copy in copies:
        copy.wait()

    row_ids = lax.broadcasted_iota(jnp.int32, (pad, pad), 0)
    col_ids = lax.broadcasted_iota(jnp.int32, (pad, pad), 1)

    def left_product(block):
        sector = left_ref[block]
        live = (row_ids < ldim_ref[sector]) & (col_ids < rdim_ref[right_ref[block]])
        state = jnp.where(live, theta[block].astype(jnp.float32), 0.0).astype(jnp.bfloat16)
        local = sector % sectors
        stack = jnp.concatenate([lenv[term, local] for term in range(terms)], axis=0)
        product = jnp.dot(stack, state, preferred_element_type=jnp.float32)
        for term in range(terms):
            scaled = product[term * pad:(term + 1) * pad] * weight_ref[term, block]
            part[block, :, term * pad:(term + 1) * pad] = scaled.astype(jnp.bfloat16)

    unroll = 2 if early % 2 == 0 and late % 2 == 0 else 1

    def each(count, body, first=0):
        def step(index, carry):
            for inner in range(unroll):
                body(first + index * unroll + inner)
            return carry
        lax.fori_loop(0, count // unroll, step, 0)

    def arrive(distance, term):
        for way, step in ((0, 1), (1, -1)):
            owner = me - step * distance
            @pl.when((owner >= 0) & (owner < owners) & (owner != last_of(me)))
            def _():
                hop(near.at[me, term], near.at[owner, term], way, distance - 1, term, step).wait_recv()
                if distance < owners - 1:
                    pass_on(near.at[owner, term], owner, way, distance, term, step)

    def arrive_far(distance, term):
        for way, step in ((0, 1), (1, -1)):
            owner = me - step * distance
            @pl.when((owner >= 0) & (owner < owners) & (owner == last_of(me)))
            def _():
                hop(near.at[me, term], far[term], way, distance - 1, term, step).wait_recv()
                if distance < owners - 1:
                    pass_on(far[term], owner, way, distance, term, step)

    cuts = [blocks * term // terms // unroll * unroll for term in range(terms)] + [blocks]
    for term in range(terms):
        each(cuts[term + 1] - cuts[term], left_product, cuts[term])
        arrive(1, term)
        arrive_far(1, term)

    def is_late(block):
        return (place_ref[right_ref[block]] // sectors == last_of(me)).astype(jnp.int32)

    late_total = lax.fori_loop(0, blocks, lambda block, count: count + is_late(block), 0)

    def rank(block, late_before):
        flag = is_late(block)
        inverse_ref[block] = jnp.where(
            flag == 1, blocks - late_total + late_before, block - late_before
        )
        return late_before + flag

    lax.fori_loop(0, blocks, rank, 0)

    def invert(slot, carry):
        found = 0
        for block in range(blocks):
            found += jnp.where(inverse_ref[block] == slot, block, 0)
        perm_ref[slot] = found
        return carry

    lax.fori_loop(0, blocks, invert, 0)

    for distance in range(2, owners - 1):
        for term in range(terms):
            arrive(distance, term)
            if distance < owners - 1:
                arrive_far(distance, term)

    def near_product(slot):
        block = perm_ref[slot]
        storage = place_ref[right_ref[block]]
        owner = storage // sectors
        sub = storage % sectors
        owner = jnp.where(owner == last_of(me), me, owner)
        stack = jnp.concatenate([near[owner, term, sub] for term in range(terms)], axis=0)
        return jnp.dot(part[block], stack, preferred_element_type=jnp.float32)

    halves = term_devices // 2
    far_half, core = mine // 2, mine % 2

    def put(group, slot, value):
        rounded = value.astype(jnp.bfloat16)
        for device in range(term_devices):
            give[group][device % 2, slot - groups[group][0], device // 2] = rounded[device * rows:(device + 1) * rows]

    def swap(first, count, group):
        return pltpu.make_async_remote_copy(
            src_ref=give[group].at[1 - core],
            dst_ref=pair[group],
            send_sem=share_send.at[group, 0],
            recv_sem=share_recv.at[group, 0],
            device_id={"term": far_half * 2 + 1 - core},
            device_id_type=MESH,
        )

    def share(first, count, group, peer):
        return pltpu.make_async_remote_copy(
            src_ref=mid[group].at[peer],
            dst_ref=take.at[peer, pl.ds(first, count)],
            send_sem=share_send.at[group, peer],
            recv_sem=share_recv.at[group, peer],
            device_id={"term": (far_half + peer) % halves * 2 + core},
            device_id_type=MESH,
        )

    def cross(group):
        first, count = groups[group]
        swap(first, count, group).wait_recv()
        for peer in range(halves):
            other = (far_half + peer) % halves
            value = give[group][core, :, other].astype(jnp.float32) + pair[group][:, other].astype(jnp.float32)
            if peer:
                mid[group][peer] = value.astype(jnp.bfloat16)
                share(first, count, group, peer).start()
            else:
                own[pl.ds(first, count)] = value

    def pieces(first, count):
        cut = 3 if count % 6 == 0 else 1
        return [(first + i * (count // cut), count // cut) for i in range(cut)]

    groups = pieces(0, early) + pieces(early, late)
    early_groups = len(pieces(0, early))

    for group in range(early_groups):
        first, count = groups[group]
        each(count, lambda slot: put(group, slot, near_product(slot)), first)
        swap(first, count, group).start()

    def keep(slot):
        total[slot - early] = near_product(slot)

    each(late, keep, early)
    for group in range(early_groups):
        cross(group)

    def far_product(slot, term):
        block = perm_ref[slot]
        storage = place_ref[right_ref[block]]
        here = storage // sectors == last_of(me)
        sub = storage % sectors
        value = jnp.dot(
            part[block, :, term * pad:(term + 1) * pad], far[term][sub], preferred_element_type=jnp.float32
        )
        held = total[slot - early]
        added = value if term == 0 else held + value
        return jnp.where(here, added, held)

    for term in range(terms):
        arrive_far(owners - 1, term)
        if term < terms - 1:
            def add(slot, term=term):
                total[slot - early] = far_product(slot, term)
            each(late, add, early)
    for group in range(early_groups, len(groups)):
        first, count = groups[group]
        each(count, lambda slot: put(group, slot, far_product(slot, terms - 1)), first)
        swap(first, count, group).start()
        if group > early_groups:
            cross(group - 1)
    cross(len(groups) - 1)

    for group, (first, count) in enumerate(groups):
        for peer in range(1, halves):
            share(first, count, group, peer).wait_recv()

    out_rows = lax.broadcasted_iota(jnp.int32, (rows, pad), 0) + mine * rows
    out_cols = lax.broadcasted_iota(jnp.int32, (rows, pad), 1)

    def finish(block):
        slot = inverse_ref[block]
        value = own[slot]
        for peer in range(1, halves):
            value = value + take[peer, slot].astype(jnp.float32)
        live = (out_rows < ldim_ref[left_ref[block]]) & (out_cols < rdim_ref[right_ref[block]])
        out_ref[block] = jnp.where(live, value, 0.0)

    each(blocks, finish)

    for group, (first, count) in enumerate(groups):
        swap(first, count, group).wait_send()
        for peer in range(1, halves):
            share(first, count, group, peer).wait_send()
    for distance in range(owners - 1):
        for term in range(terms):
            for way, step in ((0, 1), (1, -1)):
                origin = me - step * distance
                @pl.when((origin >= 0) & (origin < owners) & (me + step >= 0) & (me + step < owners))
                def _():
                    hop(near.at[me, term], near.at[me, term], way, distance, term, step).wait_send()


def shards(
    wavefunction,
    term_weights,
    left_environment,
    right_environment,
    left_sector,
    right_sector,
    right_place,
    left_dims,
    right_dims,
):
    blocks, pad, _ = wavefunction.shape
    terms, sectors = left_environment.shape[:2]
    owners = lax.axis_size("sector")
    term_devices = lax.axis_size("term")
    capacity = max(2, 2 * blocks // owners)
    if capacity < sectors or owners < 3 or term_devices % 2:
        return picked_shards(
            wavefunction,
            term_weights,
            left_environment,
            right_environment,
            left_sector,
            right_sector,
            right_place,
            left_dims,
            right_dims,
        )
    early = blocks - capacity
    rows = pad // term_devices
    hbm = pl.BlockSpec(memory_space=pltpu.HBM)
    smalls = (left_sector, right_sector, right_place, left_dims, right_dims, term_weights)
    bf16 = jnp.bfloat16
    counts = [n // cut for n in (early, capacity) for cut in (3 if n % 6 == 0 else 1,) for _ in range(cut)]
    groups = len(counts)
    return pl.pallas_call(
        functools.partial(chain_kernel, owners, term_devices, early),
        out_shape=jax.ShapeDtypeStruct((blocks, rows, pad), jnp.float32),
        in_specs=[hbm] * 9,
        out_specs=pl.BlockSpec(memory_space=pltpu.VMEM),
        scratch_shapes=[
            *[pltpu.SMEM(small.shape, small.dtype) for small in smalls],
            pltpu.SMEM((blocks,), jnp.int32),
            pltpu.SMEM((blocks,), jnp.int32),
            pltpu.VMEM((blocks, pad, pad), bf16),
            pltpu.VMEM((terms, sectors, pad, pad), bf16),
            pltpu.VMEM((owners, terms, sectors, pad, pad), bf16),
            *[pltpu.VMEM((sectors, pad, pad), bf16) for _ in range(terms)],
            pltpu.VMEM((blocks, pad, terms * pad), bf16),
            pltpu.VMEM((capacity, pad, pad), jnp.float32),
            pltpu.VMEM((blocks, rows, pad), jnp.float32),
            pltpu.VMEM((term_devices // 2, blocks, rows, pad), bf16),
            pltpu.SemaphoreType.DMA((9,)),
            pltpu.SemaphoreType.DMA((2, owners - 1, terms)),
            pltpu.SemaphoreType.DMA((2, owners - 1, terms)),
            pltpu.SemaphoreType.DMA((groups, term_devices // 2)),
            pltpu.SemaphoreType.DMA((groups, term_devices // 2)),
            *[
                pltpu.VMEM(shape, bf16)
                for count in counts
                for shape in (
                    (2, count, term_devices // 2, rows, pad),
                    (count, term_devices // 2, rows, pad),
                    (term_devices // 2, count, rows, pad),
                )
            ],
        ],
        compiler_params=pltpu.CompilerParams(
            collective_id=0, has_side_effects=True, vmem_limit_bytes=32 * 1024 * 1024
        ),
        cost_estimate=pl.CostEstimate(
            flops=4 * blocks * terms * pad**3, bytes_accessed=4 * blocks * pad * pad, transcendentals=0
        ),
    )(*smalls, wavefunction, left_environment, right_environment)


def solution(mesh):
    return jax.shard_map(
        shards,
        mesh=mesh,
        in_specs=(
            P(("groups", "sector"), None, None),
            P(("groups", "term"), "sector"),
            P(("groups", "term"), "sector", None, None),
            P(("groups", "term"), "sector", None, None),
            P(("groups", "sector")),
            P(("groups", "sector")),
            P("groups"),
            P("groups"),
            P("groups"),
        ),
        out_specs=P(("groups", "sector"), "term", None),
        check_vma=False,
    )
```

```python
import functools

import jax
import jax.numpy as jnp
from jax import lax
from jax.experimental import pallas as pl
from jax.experimental.pallas import tpu as pltpu
from jax.sharding import PartitionSpec as P


def lookup(values_table, indices):
    matches = indices[:, None] == jnp.arange(values_table.shape[0])[None, :]
    return jnp.sum(jnp.where(matches, values_table[None, :], 0), axis=1)


def picked_shards(
    wavefunction,
    term_weights,
    left_environment,
    right_environment,
    left_sector,
    right_sector,
    right_place,
    left_dims,
    right_dims,
):
    block_count = wavefunction.shape[0]
    pad_size = wavefunction.shape[1]
    term_count = left_environment.shape[0]
    sector_count = left_environment.shape[1]
    owners = lax.axis_size("sector")
    own_index = lax.axis_index("sector")
    term_devices = lax.axis_size("term")
    capacity = max(2, 2 * block_count // owners)
    part_rows = pad_size // term_devices
    row_start = lax.axis_index("term") * part_rows
    columns = jnp.arange(pad_size)
    row_live = columns[None, :] < lookup(left_dims, left_sector)[:, None]
    col_live = columns[None, :] < lookup(right_dims, right_sector)[:, None]
    live_mask = row_live[:, :, None] & col_live[:, None, :]
    masked = jnp.where(live_mask, wavefunction, jnp.zeros_like(wavefunction))
    local_left = left_sector - own_index * sector_count
    env_rows = jnp.take(jnp.transpose(left_environment, (1, 0, 2, 3)), local_left, axis=0)
    left_part = jnp.einsum("bwij,bjk->bwik", env_rows, masked, preferred_element_type=jnp.float32)
    left_part = (left_part * jnp.transpose(term_weights)[:, :, None, None]).astype(jnp.bfloat16)
    storage = lookup(right_place, right_sector)
    target = storage // sector_count
    local_right = storage % sector_count
    right_by_slot = jnp.transpose(right_environment, (1, 0, 2, 3))
    all_place = lax.all_gather(storage, "sector", axis=0, tiled=True).reshape(owners, block_count)
    owned_here = all_place // sector_count == own_index
    sub_index = all_place % sector_count
    sector_ids = jnp.arange(sector_count)
    used_here = jnp.any(
        owned_here[:, :, None] & (sub_index[:, :, None] == sector_ids[None, None, :]), axis=1
    )
    reply_cap = min(capacity, sector_count)
    used_rank = jnp.cumsum(used_here.astype(jnp.int32), axis=1) - 1
    picked = used_here[:, None, :] & (used_rank[:, None, :] == jnp.arange(reply_cap)[None, :, None])
    chosen = jnp.sum(jnp.where(picked, sector_ids[None, None, :], 0), axis=2)
    valid_slot = jnp.any(picked, axis=2)
    outgoing = jnp.take(right_by_slot, chosen.reshape(-1), axis=0)
    outgoing = outgoing.reshape(owners, reply_cap, term_count, pad_size, pad_size)
    outgoing = jnp.where(valid_slot[:, :, None, None, None], outgoing, jnp.zeros_like(outgoing))
    incoming = lax.all_to_all(outgoing, "sector", split_axis=0, concat_axis=0, tiled=True)
    own_used = jnp.any(
        (target[:, None, None] == jnp.arange(owners)[None, :, None])
        & (local_right[:, None, None] == sector_ids[None, None, :]),
        axis=0,
    )
    own_rank = jnp.cumsum(own_used.astype(jnp.int32), axis=1) - 1
    reply_index = lookup(own_rank.reshape(-1), target * sector_count + local_right)
    env_cols = jnp.take(
        incoming.reshape(owners * reply_cap, term_count, pad_size, pad_size),
        target * reply_cap + reply_index,
        axis=0,
    )
    partial_value = jnp.einsum(
        "bwij,bwjk->bik", left_part, env_cols, preferred_element_type=jnp.float32
    ).astype(jnp.bfloat16)
    shares = lax.all_to_all(
        partial_value.reshape(block_count, term_devices, part_rows, pad_size),
        "term",
        split_axis=1,
        concat_axis=1,
        tiled=True,
    )
    result = jnp.sum(shares.astype(jnp.float32), axis=1)
    row_part = lax.dynamic_slice_in_dim(live_mask, row_start, part_rows, 1)
    return jnp.where(row_part, result, jnp.zeros_like(result))


MESH = pl.DeviceIdType.MESH


def chain_kernel(
    owners,
    term_devices,
    early,
    left_hbm,
    right_hbm,
    place_hbm,
    ldim_hbm,
    rdim_hbm,
    weight_hbm,
    theta_hbm,
    lenv_hbm,
    renv_hbm,
    out_ref,
    left_ref,
    right_ref,
    place_ref,
    ldim_ref,
    rdim_ref,
    weight_ref,
    perm_ref,
    inverse_ref,
    theta,
    lenv,
    near,
    *rest,
):
    terms, sectors, pad = renv_hbm.shape[0], renv_hbm.shape[1], renv_hbm.shape[2]
    far = rest[:terms]
    (part, total, own, take, local_sem, gather_send, gather_recv, share_send, share_recv) = rest[terms:terms + 9]
    buffers = rest[terms + 9:]
    give, pair, mid = buffers[0::3], buffers[1::3], buffers[2::3]
    blocks = theta_hbm.shape[0]
    late = blocks - early
    rows = pad // term_devices
    me = lax.axis_index("sector")
    mine = lax.axis_index("term")

    def last_of(device):
        return (owners - 1) * (1 - (2 * device) // owners)

    barrier = pltpu.get_barrier_semaphore()
    for step in (-1, 1):
        @pl.when((me + step >= 0) & (me + step < owners))
        def _():
            pl.semaphore_signal(barrier, inc=1, device_id={"sector": me + step}, device_id_type=MESH)
    peers = [mine // 2 * 2 + 1 - mine % 2] + [(mine + 2 * i) % term_devices for i in range(1, term_devices // 2)]
    for peer in peers:
        pl.semaphore_signal(barrier, inc=1, device_id={"term": peer}, device_id_type=MESH)
    neighbours = (me + owners - 1) // owners + (2 * owners - 2 - me) // owners
    pl.semaphore_wait(barrier, len(peers) + neighbours)

    def hop(src, dst, way, distance, term, step):
        return pltpu.make_async_remote_copy(
            src_ref=src,
            dst_ref=dst,
            send_sem=gather_send.at[way, distance, term],
            recv_sem=gather_recv.at[way, distance, term],
            device_id={"sector": me + step},
            device_id_type=MESH,
        )

    def pass_on(src, owner, way, distance, term, step):
        target = me + step

        @pl.when((target >= 0) & (target < owners) & (owner != last_of(target)))
        def _():
            hop(src, near.at[owner, term], way, distance, term, step).start()

        @pl.when((target >= 0) & (target < owners) & (owner == last_of(target)))
        def _():
            hop(src, far[term], way, distance, term, step).start()

    for term in range(terms):
        for way, step in ((0, 1), (1, -1)):
            pass_on(renv_hbm.at[term], me, way, 0, term, step)
    copies = [
        pltpu.make_async_copy(src, dst, local_sem.at[index])
        for index, (src, dst) in enumerate((
            (left_hbm, left_ref),
            (right_hbm, right_ref),
            (place_hbm, place_ref),
            (ldim_hbm, ldim_ref),
            (rdim_hbm, rdim_ref),
            (weight_hbm, weight_ref),
            (theta_hbm, theta),
            (lenv_hbm, lenv),
            (renv_hbm, near.at[me]),
        ))
    ]
    for copy in copies:
        copy.start()
    for copy in copies:
        copy.wait()

    row_ids = lax.broadcasted_iota(jnp.int32, (pad, pad), 0)
    col_ids = lax.broadcasted_iota(jnp.int32, (pad, pad), 1)

    def left_product(block):
        sector = left_ref[block]
        live = (row_ids < ldim_ref[sector]) & (col_ids < rdim_ref[right_ref[block]])
        state = jnp.where(live, theta[block].astype(jnp.float32), 0.0).astype(jnp.bfloat16)
        local = sector % sectors
        stack = jnp.concatenate([lenv[term, local] for term in range(terms)], axis=0)
        product = jnp.dot(stack, state, preferred_element_type=jnp.float32)
        for term in range(terms):
            scaled = product[term * pad:(term + 1) * pad] * weight_ref[term, block]
            part[block, :, term * pad:(term + 1) * pad] = scaled.astype(jnp.bfloat16)

    unroll = 2 if early % 2 == 0 and late % 2 == 0 else 1

    def each(count, body, first=0):
        def step(index, carry):
            for inner in range(unroll):
                body(first + index * unroll + inner)
            return carry
        lax.fori_loop(0, count // unroll, step, 0)

    def arrive(distance, term):
        for way, step in ((0, 1), (1, -1)):
            owner = me - step * distance
            @pl.when((owner >= 0) & (owner < owners) & (owner != last_of(me)))
            def _():
                hop(near.at[me, term], near.at[owner, term], way, distance - 1, term, step).wait_recv()
                if distance < owners - 1:
                    pass_on(near.at[owner, term], owner, way, distance, term, step)

    def arrive_far(distance, term):
        for way, step in ((0, 1), (1, -1)):
            owner = me - step * distance
            @pl.when((owner >= 0) & (owner < owners) & (owner == last_of(me)))
            def _():
                hop(near.at[me, term], far[term], way, distance - 1, term, step).wait_recv()
                if distance < owners - 1:
                    pass_on(far[term], owner, way, distance, term, step)

    cuts = [blocks * term // terms // unroll * unroll for term in range(terms)] + [blocks]
    for term in range(terms):
        each(cuts[term + 1] - cuts[term], left_product, cuts[term])
        arrive(1, term)
        arrive_far(1, term)

    def is_late(block):
        return (place_ref[right_ref[block]] // sectors == last_of(me)).astype(jnp.int32)

    late_total = lax.fori_loop(0, blocks, lambda block, count: count + is_late(block), 0)

    def rank(block, late_before):
        flag = is_late(block)
        inverse_ref[block] = jnp.where(
            flag == 1, blocks - late_total + late_before, block - late_before
        )
        return late_before + flag

    lax.fori_loop(0, blocks, rank, 0)

    def invert(slot, carry):
        found = 0
        for block in range(blocks):
            found += jnp.where(inverse_ref[block] == slot, block, 0)
        perm_ref[slot] = found
        return carry

    lax.fori_loop(0, blocks, invert, 0)

    for distance in range(2, owners - 1):
        for term in range(terms):
            arrive(distance, term)
            if distance < owners - 1:
                arrive_far(distance, term)

    def near_product(slot):
        block = perm_ref[slot]
        storage = place_ref[right_ref[block]]
        owner = storage // sectors
        sub = storage % sectors
        owner = jnp.where(owner == last_of(me), me, owner)
        stack = jnp.concatenate([near[owner, term, sub] for term in range(terms)], axis=0)
        return jnp.dot(part[block], stack, preferred_element_type=jnp.float32)

    halves = term_devices // 2
    far_half, core = mine // 2, mine % 2

    def put(group, slot, value):
        rounded = value.astype(jnp.bfloat16)
        for device in range(term_devices):
            give[group][device % 2, slot - groups[group][0], device // 2] = rounded[device * rows:(device + 1) * rows]

    def swap(first, count, group):
        return pltpu.make_async_remote_copy(
            src_ref=give[group].at[1 - core],
            dst_ref=pair[group],
            send_sem=share_send.at[group, 0],
            recv_sem=share_recv.at[group, 0],
            device_id={"term": far_half * 2 + 1 - core},
            device_id_type=MESH,
        )

    def share(first, count, group, peer):
        return pltpu.make_async_remote_copy(
            src_ref=mid[group].at[peer],
            dst_ref=take.at[peer, pl.ds(first, count)],
            send_sem=share_send.at[group, peer],
            recv_sem=share_recv.at[group, peer],
            device_id={"term": (far_half + peer) % halves * 2 + core},
            device_id_type=MESH,
        )

    def cross(group):
        first, count = groups[group]
        swap(first, count, group).wait_recv()
        for peer in range(halves):
            other = (far_half + peer) % halves
            value = give[group][core, :, other].astype(jnp.float32) + pair[group][:, other].astype(jnp.float32)
            if peer:
                mid[group][peer] = value.astype(jnp.bfloat16)
                share(first, count, group, peer).start()
            else:
                own[pl.ds(first, count)] = value

    def pieces(first, count):
        cut = 3 if count % 6 == 0 else 1
        return [(first + i * (count // cut), count // cut) for i in range(cut)]

    groups = pieces(0, early) + pieces(early, late)
    early_groups = len(pieces(0, early))

    for group in range(early_groups):
        first, count = groups[group]
        each(count, lambda slot: put(group, slot, near_product(slot)), first)
        swap(first, count, group).start()

    def keep(slot):
        total[slot - early] = near_product(slot)

    each(late, keep, early)
    for group in range(early_groups):
        cross(group)

    def far_product(slot, term):
        block = perm_ref[slot]
        storage = place_ref[right_ref[block]]
        here = storage // sectors == last_of(me)
        sub = storage % sectors
        value = jnp.dot(
            part[block, :, term * pad:(term + 1) * pad], far[term][sub], preferred_element_type=jnp.float32
        )
        held = total[slot - early]
        added = value if term == 0 else held + value
        return jnp.where(here, added, held)

    for term in range(terms):
        arrive_far(owners - 1, term)
        if term < terms - 1:
            def add(slot, term=term):
                total[slot - early] = far_product(slot, term)
            each(late, add, early)
    for group in range(early_groups, len(groups)):
        first, count = groups[group]
        each(count, lambda slot: put(group, slot, far_product(slot, terms - 1)), first)
        swap(first, count, group).start()
        if group > early_groups:
            cross(group - 1)
    cross(len(groups) - 1)

    for group, (first, count) in enumerate(groups):
        for peer in range(1, halves):
            share(first, count, group, peer).wait_recv()

    out_rows = lax.broadcasted_iota(jnp.int32, (rows, pad), 0) + mine * rows
    out_cols = lax.broadcasted_iota(jnp.int32, (rows, pad), 1)

    def finish(block):
        slot = inverse_ref[block]
        value = own[slot]
        for peer in range(1, halves):
            value = value + take[peer, slot].astype(jnp.float32)
        live = (out_rows < ldim_ref[left_ref[block]]) & (out_cols < rdim_ref[right_ref[block]])
        out_ref[block] = jnp.where(live, value, 0.0)

    each(blocks, finish)

    for group, (first, count) in enumerate(groups):
        swap(first, count, group).wait_send()
        for peer in range(1, halves):
            share(first, count, group, peer).wait_send()
    for distance in range(owners - 1):
        for term in range(terms):
            for way, step in ((0, 1), (1, -1)):
                origin = me - step * distance
                @pl.when((origin >= 0) & (origin < owners) & (me + step >= 0) & (me + step < owners))
                def _():
                    hop(near.at[me, term], near.at[me, term], way, distance, term, step).wait_send()


def shards(
    wavefunction,
    term_weights,
    left_environment,
    right_environment,
    left_sector,
    right_sector,
    right_place,
    left_dims,
    right_dims,
):
    blocks, pad, _ = wavefunction.shape
    terms, sectors = left_environment.shape[:2]
    owners = lax.axis_size("sector")
    term_devices = lax.axis_size("term")
    capacity = max(2, 2 * blocks // owners)
    if capacity < sectors or owners < 3 or term_devices % 2:
        return picked_shards(
            wavefunction,
            term_weights,
            left_environment,
            right_environment,
            left_sector,
            right_sector,
            right_place,
            left_dims,
            right_dims,
        )
    early = blocks - capacity
    rows = pad // term_devices
    hbm = pl.BlockSpec(memory_space=pltpu.HBM)
    smalls = (left_sector, right_sector, right_place, left_dims, right_dims, term_weights)
    bf16 = jnp.bfloat16
    counts = [n // cut for n in (early, capacity) for cut in (3 if n % 6 == 0 else 1,) for _ in range(cut)]
    groups = len(counts)
    return pl.pallas_call(
        functools.partial(chain_kernel, owners, term_devices, early),
        out_shape=jax.ShapeDtypeStruct((blocks, rows, pad), jnp.float32),
        in_specs=[hbm] * 9,
        out_specs=pl.BlockSpec(memory_space=pltpu.VMEM),
        scratch_shapes=[
            *[pltpu.SMEM(small.shape, small.dtype) for small in smalls],
            pltpu.SMEM((blocks,), jnp.int32),
            pltpu.SMEM((blocks,), jnp.int32),
            pltpu.VMEM((blocks, pad, pad), bf16),
            pltpu.VMEM((terms, sectors, pad, pad), bf16),
            pltpu.VMEM((owners, terms, sectors, pad, pad), bf16),
            *[pltpu.VMEM((sectors, pad, pad), bf16) for _ in range(terms)],
            pltpu.VMEM((blocks, pad, terms * pad), bf16),
            pltpu.VMEM((capacity, pad, pad), jnp.float32),
            pltpu.VMEM((blocks, rows, pad), jnp.float32),
            pltpu.VMEM((term_devices // 2, blocks, rows, pad), bf16),
            pltpu.SemaphoreType.DMA((9,)),
            pltpu.SemaphoreType.DMA((2, owners - 1, terms)),
            pltpu.SemaphoreType.DMA((2, owners - 1, terms)),
            pltpu.SemaphoreType.DMA((groups, term_devices // 2)),
            pltpu.SemaphoreType.DMA((groups, term_devices // 2)),
            *[
                pltpu.VMEM(shape, bf16)
                for count in counts
                for shape in (
                    (2, count, term_devices // 2, rows, pad),
                    (count, term_devices // 2, rows, pad),
                    (term_devices // 2, count, rows, pad),
                )
            ],
        ],
        compiler_params=pltpu.CompilerParams(
            collective_id=0, has_side_effects=True, vmem_limit_bytes=56 * 1024 * 1024
        ),
        cost_estimate=pl.CostEstimate(
            flops=4 * blocks * terms * pad**3, bytes_accessed=4 * blocks * pad * pad, transcendentals=0
        ),
    )(*smalls, wavefunction, left_environment, right_environment)


def solution(mesh):
    return jax.shard_map(
        shards,
        mesh=mesh,
        in_specs=(
            P(("groups", "sector"), None, None),
            P(("groups", "term"), "sector"),
            P(("groups", "term"), "sector", None, None),
            P(("groups", "term"), "sector", None, None),
            P(("groups", "sector")),
            P(("groups", "sector")),
            P("groups"),
            P("groups"),
            P("groups"),
        ),
        out_specs=P(("groups", "sector"), "term", None),
        check_vma=False,
    )
```
